32 devices in a mesh: groups: 2 (over x), pool: 1, tensor: 16 (over z, y, core).
Axes of the slice: x: 2, y: 2, z: 4, core: 2. Of those that a mesh axis runs over, the one named last changes fastest.
Arguments:
- hidden_state: bfloat16 [128, 8192], P(('groups', 'pool', 'tensor')), parts along dimension 0, may hold values from -6 to 6
- query_weight: bfloat16 [8192, 8192], P(None, 'tensor'), may hold values from -0.0625 to 0.0625
- keyval_weight: bfloat16 [8192, 2048], P(None, 'tensor'), may hold values from -0.0625 to 0.0625
- output_weight: bfloat16 [8192, 8192], P('tensor'), may hold values from -0.0625 to 0.0625
- cache_entries: bfloat16 [128, 48, 8, 256], P(('groups', 'pool', 'tensor')), parts along dimension 0, may hold values from -256 to 256
- adapter_pool: bfloat16 [64, 4, 16, 8192], P(('groups', 'pool', 'tensor')), parts along dimension 0, may hold values from -3 to 3
- page_table: int32 [64], P('groups'), parts along dimension 0, may hold values from 0 to 31, as said below
- fetch_list: int32 [64], P('groups'), parts along dimension 0, may hold values from 0 to 31, as said below
- row_tenant: int32 [128], P(('groups', 'pool')), parts along dimension 0, may hold values from 0 to 31, as said below
- cache_length: int32 [128], P(('groups', 'pool', 'tensor')), parts along dimension 0, may hold values from 1 to 46, as said below
Outputs:
- updates: bfloat16 [2, 128, 8192], P(None, ('groups', 'pool', 'tensor')), parts along dimension 1
The draws below stay inside these ranges and needn't reach their ends.
There are 2 independent parts, one for each index of `groups`. The reference program is written for one: setup_inputs(seed, part) draws one part's arguments, and reference() takes and returns one part's arrays. A program takes and returns all parts, laid end to end along the dimension named above; an argument that names none is the same for every part. Nothing has to cross between parts.
Inputs may be any that keep to these rules, and one draw needn't show every extreme that they name: `fetch_list`: 32 different tenants. `page_table`: a one-to-one map of tenants to pages; page p lies on the device of index p // 2 over pool and tensor (pool index major), in its local slot p % 2; no device holds the pages of more than 2 fetched tenants, and some device holds exactly 2. `row_tenant`: every row's tenant is in fetch_list; in the rows of each index of pool every fetched tenant has some row. `cache_length`: some row has exactly 46.
All inputs are finite; a program needn't handle non-finite values.
Results may differ from the reference program's by a relative error of at most 0.035.
Values may be sent and summed in bfloat16 or wider, within the bound.
A program may use at most 128 MiB of HBM per device.

```python
import jax
import jax.numpy as jnp
from jax import lax

D = 8192
HEADS = 64
KVH = 8
HD = 128
R = 16
FETCH = 32
SLOTS = 2
CTX = 48
KVF = 2048
OWNERS = 16
PAGES = 32
TENANTS = 32
OWN_MAX = 2
ROWS = 64


def fetch_plan(key):
    subkeys = jax.random.split(key, 6)
    device_order = jax.random.permutation(subkeys[0], OWNERS).astype(jnp.int32)
    leader = device_order[0]
    others = jnp.repeat(device_order[1:], OWN_MAX)
    picked = jax.random.permutation(subkeys[1], others)[:FETCH - OWN_MAX]
    owners = jnp.concatenate([jnp.full((OWN_MAX,), leader, jnp.int32), picked.astype(jnp.int32)])
    owners = jax.random.permutation(subkeys[2], owners)
    fetch_index = jnp.arange(FETCH, dtype=jnp.int32)
    earlier = (owners[:, None] == owners[None, :]) & (fetch_index[None, :] < fetch_index[:, None])
    owner_rank = jnp.sum(earlier.astype(jnp.int32), axis=1)
    shifts = jax.random.randint(subkeys[3], (OWNERS,), 0, SLOTS)
    slot_of = (jnp.take(shifts, owners) + owner_rank) % SLOTS
    fetched_pages = owners * SLOTS + slot_of
    tenant_order = jax.random.permutation(subkeys[4], TENANTS).astype(jnp.int32)
    fetch_ids = tenant_order[:FETCH]
    hits = fetched_pages[:, None] == jnp.arange(PAGES, dtype=jnp.int32)[None, :]
    hit_any = jnp.any(hits, axis=0)
    position = jnp.sum(jnp.where(hits, fetch_index[:, None], 0), axis=0)
    filler = FETCH + jax.random.permutation(subkeys[5], PAGES).astype(jnp.int32)
    sort_score = jnp.where(hit_any, position, filler)
    page_order = jnp.argsort(sort_score, stable=True).astype(jnp.int32)
    page_map = jnp.zeros((TENANTS,), jnp.int32).at[tenant_order].set(page_order)
    return (fetch_ids, page_map)


def draw_fetch_list(key, part):
    fetch_ids, page_map = fetch_plan(key)
    return fetch_ids


def draw_page_table(key, part):
    fetch_ids, page_map = fetch_plan(key)
    return page_map


def draw_row_tenant(key, part):
    fetch_ids, page_map = fetch_plan(key)
    key = jax.random.fold_in(key, 13)
    subkeys = jax.random.split(key, 3)
    row_index = jnp.arange(ROWS, dtype=jnp.int32)
    cover = jax.random.permutation(subkeys[0], FETCH).astype(jnp.int32)
    spread = jnp.take(cover, row_index // 2 % FETCH)
    first_draw = jax.random.randint(subkeys[1], (ROWS,), 0, FETCH)
    second_draw = jax.random.randint(subkeys[2], (ROWS,), 0, FETCH)
    skewed = first_draw * second_draw // FETCH
    chosen = jnp.where(row_index % 2 == 0, spread, skewed)
    return jnp.take(fetch_ids, chosen).astype(jnp.int32)


def draw_cache_length(key, part):
    key = jax.random.fold_in(key, 14)
    subkeys = jax.random.split(key, 2)
    lengths = jax.random.randint(subkeys[0], (ROWS,), 1, CTX - 1)
    longest = jax.random.randint(subkeys[1], (), 0, ROWS)
    lengths = jnp.where(jnp.arange(ROWS) == longest, CTX - 2, lengths)
    return lengths.astype(jnp.int32)


def draw_cache_entries(key, part):
    key = jax.random.fold_in(key, 15)
    subkeys = jax.random.split(key, 2)
    values = jnp.clip(jax.random.normal(subkeys[0], (ROWS, CTX, KVH, HD), jnp.float32), -6.0, 6.0)
    key_part = jnp.clip(jax.random.normal(subkeys[1], (ROWS, CTX, KVH, HD), jnp.float32), -6.0, 6.0)
    return jnp.concatenate([key_part, values], axis=-1).astype(jnp.bfloat16)


def draw_adapter_pool(key, part):
    key = jax.random.fold_in(key, 16)
    scales = jnp.array([D ** (-0.5), R ** (-0.5), D ** (-0.5), R ** (-0.5)], jnp.float32).reshape(1, 4, 1, 1)
    entries = jnp.clip(jax.random.normal(key, (PAGES, 4, R, D), jnp.float32), -6.0, 6.0)
    return (entries * scales).astype(jnp.bfloat16)


def levels(key, dims, cuts, low, top_value):
    level, own = 1.0, jax.random.fold_in(key, 6)
    for dim, shards_of in cuts:
        draws = jnp.exp(jax.random.uniform(jax.random.fold_in(own, dim), (shards_of,), jnp.float32, low / len(cuts), top_value / len(cuts)))
        level = level * jnp.repeat(draws, dims[dim] // shards_of).reshape([-1 if axis == dim else 1 for axis in range(len(dims))])
    return level


def centred(key, shape, deviation, reach, pieces=(), kind=jnp.bfloat16):
    gain = levels(key, shape, pieces, -0.22, 0.18) if pieces else 1.0
    result = jax.random.normal(key, shape, jnp.float32) * deviation * gain
    return jnp.minimum(jnp.maximum(result, -reach), reach).astype(kind)


def setup_inputs(seed: int = 0, part: int = 0) -> dict:
    streams_of = jax.random.split(jax.random.key(seed), 11)
    part_splits = jax.random.split(jax.random.fold_in(streams_of[10], part), 11)
    hidden_state = centred(part_splits[0], (ROWS, D), 1.0, 6.0, ((0, 16),))
    query_weight = centred(streams_of[1], (D, D), D ** -0.5, 0.0625, ((1, 16),))
    keyval_weight = centred(streams_of[2], (D, KVF), D ** -0.5, 0.0625, ((1, 16),))
    output_weight = centred(streams_of[3], (D, D), D ** -0.5, 0.0625, ((0, 16),))
    cache_entries = draw_cache_entries(jax.random.fold_in(jax.random.fold_in(streams_of[10], part), 71), part)
    adapter_pool = draw_adapter_pool(jax.random.fold_in(jax.random.fold_in(streams_of[10], part), 71), part)
    page_table = draw_page_table(jax.random.fold_in(jax.random.fold_in(streams_of[10], part), 71), part)
    fetch_list = draw_fetch_list(jax.random.fold_in(jax.random.fold_in(streams_of[10], part), 71), part)
    row_tenant = draw_row_tenant(jax.random.fold_in(jax.random.fold_in(streams_of[10], part), 71), part)
    cache_length = draw_cache_length(jax.random.fold_in(jax.random.fold_in(streams_of[10], part), 71), part)
    return {"hidden_state": hidden_state, "query_weight": query_weight, "keyval_weight": keyval_weight, "output_weight": output_weight, "cache_entries": cache_entries, "adapter_pool": adapter_pool, "page_table": page_table, "fetch_list": fetch_list, "row_tenant": row_tenant, "cache_length": cache_length}


rope_base = 500000.0
norm_epsilon = 1e-05

def rotate(vectors, positions):
    half_dim = vectors.shape[-1] // 2
    frequency = rope_base ** (-2.0 * jnp.arange(half_dim, dtype=jnp.float32) / vectors.shape[-1])
    angles = positions.astype(jnp.float32)[:, None] * frequency[None, :]
    cosine_term = jnp.cos(angles)[:, None, :]
    sine_term = jnp.sin(angles)[:, None, :]
    lead_half = vectors[..., :half_dim]
    trail_half = vectors[..., half_dim:]
    return jnp.concatenate([lead_half * cosine_term - trail_half * sine_term, trail_half * cosine_term + lead_half * sine_term], axis=-1)

def attend(query_rot, new_keys, new_values, cache_entries, cache_length):
    row_total = query_rot.shape[0]
    key_heads = cache_entries.shape[2]
    head_dim = query_rot.shape[2]
    group_size = query_rot.shape[1] // key_heads
    query_vectors = query_rot.reshape(row_total, key_heads, group_size, head_dim).astype(jnp.float32)
    cached_keys = cache_entries[..., :head_dim].astype(jnp.float32)
    cached_values = cache_entries[..., head_dim:].astype(jnp.float32)
    scale = float(head_dim) ** (-0.5)
    scores_cache = jnp.einsum('rhgd,rchd->rhgc', query_vectors, cached_keys) * scale
    in_length = jnp.arange(cache_entries.shape[1], dtype=jnp.int32)[None, :] < cache_length[:, None]
    scores_cache = jnp.where(in_length[:, None, None, :], scores_cache, -1e+30)
    scores_new = jnp.einsum('rhgd,rjhd->rhgj', query_vectors, new_keys.astype(jnp.float32)) * scale
    highest = jnp.maximum(lax.optimization_barrier(jnp.max(scores_cache, axis=-1)), lax.optimization_barrier(jnp.max(scores_new, axis=-1)))[..., None]
    exp_cache = jnp.exp(scores_cache - highest)
    exp_new = jnp.exp(scores_new - highest)
    denominator = lax.optimization_barrier(jnp.sum(exp_cache, axis=-1, keepdims=True)) + lax.optimization_barrier(jnp.sum(exp_new, axis=-1, keepdims=True))
    weight_cache = (exp_cache / denominator).astype(jnp.bfloat16).astype(jnp.float32)
    weight_new = (exp_new / denominator).astype(jnp.bfloat16).astype(jnp.float32)
    combined = jnp.einsum('rhgc,rchd->rhgd', weight_cache, cached_values)
    combined = combined + jnp.einsum('rhgj,rjhd->rhgd', weight_new, new_values.astype(jnp.float32))
    return combined.reshape(row_total, -1).astype(jnp.bfloat16)

def adapter_shrink(input_rows, down_adapter_tiles, tenant_selector):
    per_tenant = jnp.einsum('nd,fkd->nfk', input_rows.astype(jnp.float32), down_adapter_tiles.astype(jnp.float32))
    return lax.optimization_barrier(jnp.sum(per_tenant * tenant_selector[:, :, None], axis=1)).astype(jnp.bfloat16)

def adapter_expand(shrink_matrix, up_adapter_tiles, tenant_selector):
    spread = tenant_selector[:, :, None] * shrink_matrix.astype(jnp.float32)[:, None, :]
    return jnp.einsum('nfk,fkc->nc', spread, up_adapter_tiles.astype(jnp.float32))

def reference(hidden_state, query_weight, keyval_weight, output_weight, cache_entries, adapter_pool, page_table, fetch_list, row_tenant, cache_length):
    row_total = hidden_state.shape[0]
    matched = fetch_list[:, None] == jnp.arange(page_table.shape[0], dtype=jnp.int32)[None, :]
    page_ids = lax.optimization_barrier(jnp.sum(jnp.where(matched, page_table[None, :], 0), axis=1)).astype(jnp.int32)
    adapter_tiles = jnp.take(adapter_pool, page_ids, axis=0)
    tenant_selector = (row_tenant[:, None] == fetch_list[None, :]).astype(jnp.float32)
    residual = hidden_state
    new_keys = []
    new_values = []
    updates = []
    for step_index in range(2):
        widened = residual.astype(jnp.float32)
        normalized_input = (widened * lax.rsqrt(lax.optimization_barrier(jnp.mean(widened * widened, axis=1, keepdims=True)) + norm_epsilon)).astype(jnp.bfloat16)
        query_baseline = jnp.dot(normalized_input, query_weight, preferred_element_type=jnp.float32)
        query_reduced = adapter_shrink(normalized_input, adapter_tiles[:, 0], tenant_selector)
        query_vectors = (query_baseline + adapter_expand(query_reduced, adapter_tiles[:, 1], tenant_selector)).astype(jnp.bfloat16)
        keyval = jnp.dot(normalized_input, keyval_weight, preferred_element_type=jnp.float32).astype(jnp.bfloat16)
        keyval = keyval.reshape(row_total, KVH, 2 * HD)
        positions = cache_length + step_index
        query_rot = rotate(query_vectors.reshape(row_total, HEADS, HD).astype(jnp.float32), positions).astype(jnp.bfloat16)
        key_rot = rotate(keyval[..., :HD].astype(jnp.float32), positions).astype(jnp.bfloat16)
        new_keys.append(key_rot)
        new_values.append(keyval[..., HD:])
        attention_result = attend(query_rot, jnp.stack(new_keys, axis=1), jnp.stack(new_values, axis=1), cache_entries, cache_length)
        base_total = jnp.dot(attention_result, output_weight, preferred_element_type=jnp.float32)
        output_reduced = adapter_shrink(attention_result, adapter_tiles[:, 2], tenant_selector)
        state_update = (base_total + adapter_expand(output_reduced, adapter_tiles[:, 3], tenant_selector)).astype(jnp.bfloat16)
        updates.append(state_update)
        residual = (residual.astype(jnp.float32) + state_update.astype(jnp.float32)).astype(jnp.bfloat16)
    return jnp.stack(updates)
```

```python
import jax
import jax.numpy as jnp
from jax import lax
from jax.experimental import pallas as pl
from jax.experimental.pallas import tpu as pltpu
from jax.sharding import PartitionSpec as P

HEADS = 64
KVH = 8
HD = 128
FETCH = 32


rope_base = 500000.0
norm_epsilon = 1e-05


def rotate(vectors, positions):
    half_dim = vectors.shape[-1] // 2
    frequency = rope_base ** (-2.0 * jnp.arange(half_dim, dtype=jnp.float32) / vectors.shape[-1])
    angles = positions.astype(jnp.float32)[:, None] * frequency[None, :]
    cosine_term = jnp.cos(angles)[:, None, :]
    sine_term = jnp.sin(angles)[:, None, :]
    lead_half = vectors[..., :half_dim]
    trail_half = vectors[..., half_dim:]
    return jnp.concatenate(
        [
            lead_half * cosine_term - trail_half * sine_term,
            trail_half * cosine_term + lead_half * sine_term,
        ],
        axis=-1,
    )


def attend(query_rot, new_keys, new_values, cache_entries, cache_length):
    row_total = query_rot.shape[0]
    key_heads = cache_entries.shape[2]
    head_dim = query_rot.shape[2]
    group_size = query_rot.shape[1] // key_heads
    query_vectors = query_rot.reshape(row_total, key_heads, group_size, head_dim)
    cached_keys = cache_entries[..., :head_dim]
    cached_values = cache_entries[..., head_dim:]
    scale = float(head_dim) ** (-0.5)
    scores_cache = (
        jnp.einsum(
            "rhgd,rchd->rhgc", query_vectors, cached_keys, preferred_element_type=jnp.float32
        )
        * scale
    )
    in_length = jnp.arange(cache_entries.shape[1], dtype=jnp.int32)[None, :] < cache_length[:, None]
    scores_cache = jnp.where(in_length[:, None, None, :], scores_cache, -1e30)
    scores_new = (
        jnp.einsum("rhgd,rjhd->rhgj", query_vectors, new_keys, preferred_element_type=jnp.float32)
        * scale
    )
    highest = jnp.maximum(jnp.max(scores_cache, axis=-1), jnp.max(scores_new, axis=-1))[..., None]
    exp_cache = jnp.exp(scores_cache - highest)
    exp_new = jnp.exp(scores_new - highest)
    denominator = jnp.sum(exp_cache, axis=-1, keepdims=True) + jnp.sum(
        exp_new, axis=-1, keepdims=True
    )
    weight_cache = (exp_cache / denominator).astype(jnp.bfloat16)
    weight_new = (exp_new / denominator).astype(jnp.bfloat16)
    combined = jnp.einsum(
        "rhgc,rchd->rhgd", weight_cache, cached_values, preferred_element_type=jnp.float32
    )
    combined = combined + jnp.einsum(
        "rhgj,rjhd->rhgd", weight_new, new_values, preferred_element_type=jnp.float32
    )
    return combined.reshape(row_total, -1).astype(jnp.bfloat16)


def expand_matrix(shrink_matrix, selector_lowrank, up_adapter_tiles):
    spread = selector_lowrank[:, :, None] * shrink_matrix[:, None, :]
    return jnp.einsum("nfk,fkc->nc", spread, up_adapter_tiles, preferred_element_type=jnp.float32)


def on_device(
    hidden_state,
    query_weight,
    keyval_weight,
    output_weight,
    cache_entries,
    adapter_pool,
    page_table,
    fetch_list,
    row_tenant,
    cache_length,
):
    tensor_count = lax.axis_size("tensor")
    pool_count = lax.axis_size("pool")
    tensor_index = lax.axis_index("tensor")
    device_index = lax.axis_index("pool") * tensor_count + tensor_index
    row_count = hidden_state.shape[0]
    model_width = hidden_state.shape[1]
    block_width = model_width // tensor_count
    slot_count = adapter_pool.shape[0]
    owner_count = pool_count * tensor_count
    capacity = max(2, (FETCH + owner_count - 1) // owner_count)
    matched = fetch_list[:, None] == jnp.arange(page_table.shape[0], dtype=jnp.int32)[None, :]
    page_ids = jnp.sum(jnp.where(matched, page_table[None, :], 0), axis=1)
    owners = page_ids // slot_count
    slot_ids = page_ids % slot_count
    fetch_order = jnp.arange(FETCH, dtype=jnp.int32)
    earlier = (owners[:, None] == owners[None, :]) & (fetch_order[None, :] < fetch_order[:, None])
    owner_rank = jnp.sum(earlier.astype(jnp.int32), axis=1)
    owned_here = owners == device_index
    chosen = owned_here[None, :] & (
        owner_rank[None, :] == jnp.arange(capacity, dtype=jnp.int32)[:, None]
    )
    send_slots = jnp.sum(jnp.where(chosen, slot_ids[None, :], 0), axis=1)
    present = jnp.any(chosen, axis=1).astype(jnp.bfloat16)
    outgoing = jnp.take(adapter_pool, send_slots, axis=0) * present[:, None, None, None]
    doubled = jnp.concatenate([outgoing] * pool_count, axis=3)
    arrived = lax.all_to_all(doubled, ("pool", "tensor"), split_axis=3, concat_axis=0, tiled=True)
    adapter_tiles = jnp.take(arrived, owners * capacity + owner_rank, axis=0)
    down_query = adapter_tiles[:, 0]
    up_query = adapter_tiles[:, 1]
    down_out = adapter_tiles[:, 2]
    up_projected = adapter_tiles[:, 3]
    row_hits = row_tenant[:, None] == fetch_list[None, :]
    onehot_wide = row_hits.astype(jnp.float32)
    selector_lowrank = row_hits.astype(jnp.bfloat16)
    column_start = tensor_index * block_width
    query_cols = query_weight.shape[1]
    keyval_cols = keyval_weight.shape[1]
    residual = hidden_state
    new_keys = []
    new_values = []
    updates = []
    for step_index in range(2):
        widened = residual.astype(jnp.float32)
        normalized_input = (
            widened * lax.rsqrt(jnp.mean(widened * widened, axis=1, keepdims=True) + norm_epsilon)
        ).astype(jnp.bfloat16)
        features_part = lax.all_gather(normalized_input, "tensor", axis=0, tiled=True)
        query_baseline = jnp.dot(features_part, query_weight, preferred_element_type=jnp.float32)
        keyval = jnp.dot(features_part, keyval_weight, preferred_element_type=jnp.float32)
        own_cols = lax.dynamic_slice_in_dim(features_part, column_start, block_width, 1)
        per_tenant = jnp.einsum(
            "nd,fkd->nfk", own_cols, down_query, preferred_element_type=jnp.float32
        )
        shrink_matrix = jnp.sum(per_tenant * onehot_wide[:, :, None], axis=1)
        projected = jnp.concatenate([query_baseline, keyval, shrink_matrix], axis=1)
        shrink_query = lax.psum(projected[:, query_cols + keyval_cols :], "tensor").astype(
            jnp.bfloat16
        )
        query_vectors = (
            projected[:, :query_cols] + expand_matrix(shrink_query, selector_lowrank, up_query)
        ).astype(jnp.bfloat16)
        keyval = projected[:, query_cols : query_cols + keyval_cols].astype(jnp.bfloat16)
        query_rows, keyval_rows = (
            lax.all_to_all(query_vectors, "tensor", split_axis=0, concat_axis=1, tiled=True),
            lax.all_to_all(keyval, "tensor", split_axis=0, concat_axis=1, tiled=True),
        )
        positions = cache_length + step_index
        query_rot = rotate(
            query_rows.reshape(row_count, HEADS, HD).astype(jnp.float32), positions
        ).astype(jnp.bfloat16)
        keyval_rows = keyval_rows.reshape(row_count, KVH, 2 * HD)
        key_rot = rotate(keyval_rows[..., :HD].astype(jnp.float32), positions).astype(jnp.bfloat16)
        new_keys.append(key_rot)
        new_values.append(keyval_rows[..., HD:])
        attention_result = attend(
            query_rot,
            jnp.stack(new_keys, axis=1),
            jnp.stack(new_values, axis=1),
            cache_entries,
            cache_length,
        )
        head_rows = lax.all_to_all(
            attention_result, "tensor", split_axis=1, concat_axis=0, tiled=True
        )
        base_total = lax.psum_scatter(
            jnp.dot(head_rows, output_weight, preferred_element_type=jnp.float32),
            "tensor",
            scatter_dimension=0,
            tiled=True,
        )
        per_tenant = jnp.einsum(
            "nc,fkc->nfk", head_rows, down_out, preferred_element_type=jnp.float32
        )
        partial_out = jnp.sum(per_tenant * onehot_wide[:, :, None], axis=1)
        reduced_output = lax.psum(partial_out, "tensor").astype(jnp.bfloat16)
        adapter_columns = expand_matrix(reduced_output, selector_lowrank, up_projected)
        adapter_portion = lax.all_to_all(
            adapter_columns, "tensor", split_axis=0, concat_axis=1, tiled=True
        )
        state_update = (base_total + adapter_portion).astype(jnp.bfloat16)
        updates.append(state_update)
        residual = (residual.astype(jnp.float32) + state_update.astype(jnp.float32)).astype(
            jnp.bfloat16
        )
    return jnp.stack(updates)


DEVS = 16
OWN = 4
QUARTER = 2048
CHUNKS = 2
LANES = QUARTER // CHUNKS
KEYS = 1536
BF = jnp.bfloat16
F32 = jnp.float32


def iota(shape, dim):
    return lax.broadcasted_iota(jnp.int32, shape, dim)


def dot(a, b):
    return jnp.dot(a, b, preferred_element_type=F32)


def dot_nt(a, b):
    return lax.dot_general(a, b, (((1,), (1,)), ((), ())), preferred_element_type=F32)


def fused(
    x0, page_col, page_row, length_col, cosine, sine, wq_hbm, wkv_hbm, wo_hbm, cache_hbm, pool_hbm,
    out,
    wq, wkv, wo, aq, bo, bq, ao, kvbuf, bias, perm, perm_t, perm_q,
    x_cur, xs, xp, pb, bs, r1, s1, r2, s2, r3,
    qs_send, qs_recv, tq, q_send, q_recv, a_send, a_recv, am, os_send, os_recv,
    load_sem, ad_ss, ad_rs, agz_ss, agy_ss, agc_ss, ag_rs,
    qs_ss, qs_rs, q_ss, q_rs, a_ss, a_rs, os_ss, os_rs,
    rs1_ss, rs1_rs, rs2_ss, rs2_rs, rs3_ss, rs3_rs,
):
    me = lax.axis_index("tensor")
    z, y, c = me // 4, (me // 2) % 2, me % 2
    y_peer = z * 4 + (1 - y) * 2 + c
    c_peer = z * 4 + y * 2 + (1 - c)

    def remote(src, dst, ss, rs, peer):
        return pltpu.make_async_remote_copy(
            src_ref=src, dst_ref=dst, send_sem=ss, recv_sem=rs,
            device_id={"tensor": peer}, device_id_type=pl.DeviceIdType.MESH,
        )

    def peers(body):
        def one(i, carry):
            body(lax.rem(me + i, DEVS))
            return carry
        lax.fori_loop(1, DEVS, one, 0)

    loads = [
        pltpu.make_async_copy(pool_hbm.at[:, 0], aq, load_sem.at[0]),
        pltpu.make_async_copy(wq_hbm, wq, load_sem.at[1]),
        pltpu.make_async_copy(wkv_hbm, wkv, load_sem.at[2]),
        pltpu.make_async_copy(cache_hbm, kvbuf.at[pl.ds(0, KEYS)], load_sem.at[3]),
        pltpu.make_async_copy(wo_hbm, wo, load_sem.at[4]),
        pltpu.make_async_copy(pool_hbm.at[:, 3], bo, load_sem.at[5]),
        pltpu.make_async_copy(
            pool_hbm.at[:, 1, :, pl.ds(pl.multiple_of(me * 512, 512), 512)],
            bq.at[pl.ds(2 * me, 2)], load_sem.at[6]),
        pltpu.make_async_copy(
            pool_hbm.at[:, 2, :, pl.ds(pl.multiple_of(me * 512, 512), 512)],
            ao.at[pl.ds(2 * me, 2)], load_sem.at[7]),
    ]
    for load in loads:
        load.start()

    barrier = pltpu.get_barrier_semaphore()
    peers(lambda d: pl.semaphore_signal(
        barrier, inc=1, device_id={"tensor": d}, device_id_type=pl.DeviceIdType.MESH))
    pl.semaphore_wait(barrier, DEVS - 1)

    def ag_z(j, dz):
        zz = lax.rem(z + dz, 4)
        return remote(xs.at[j, me], xs.at[j, me], agz_ss.at[j, dz], ag_rs.at[j, me], zz * 4 + y * 2 + c)

    def ag_y(j, zz):
        b = zz * 4 + y * 2 + c
        return remote(xs.at[j, b], xs.at[j, b], agy_ss.at[j, zz], ag_rs.at[j, b], y_peer)

    def ag_c(j, zz, yy):
        b = zz * 4 + yy * 2 + c
        return remote(xs.at[j, b], xs.at[j, b], agc_ss.at[j, zz * 2 + yy], ag_rs.at[j, b], c_peer)

    def ag_wait(j, b):
        remote(xs.at[j, b], xs.at[j, b], agz_ss.at[j, 0], ag_rs.at[j, b], c_peer).wait_recv()

    def ag_begin(j):
        xs[j, me] = x_cur[j]
        for dz in (1, 2, 3):
            ag_z(j, dz).start()
        ag_y(j, z).start()
        ag_c(j, z, y).start()

    def ag_forward(j):
        for dz in (1, 2, 3):
            zz = lax.rem(z + dz, 4)
            ag_wait(j, zz * 4 + y * 2 + c)
            ag_y(j, zz).start()
            ag_c(j, zz, y).start()
        for dz in range(4):
            zz = lax.rem(z + dz, 4)
            ag_wait(j, zz * 4 + (1 - y) * 2 + c)
            ag_c(j, zz, 1 - y).start()

    def ag_finish(j):
        for b in range(8):
            ag_wait(j, b * 2 + (1 - c))

    def ag_drain(j):
        for dz in (1, 2, 3):
            ag_z(j, dz).wait_send()
        for zz in range(4):
            ag_y(j, zz).wait_send()
            for yy in range(2):
                ag_c(j, zz, yy).wait_send()

    def adapter(kind, dst, d):
        return remote(
            pool_hbm.at[:, 1 + kind, :, pl.ds(pl.multiple_of(d * 512, 512), 512)],
            dst.at[pl.ds(2 * me, 2)], ad_ss.at[kind, d], ad_rs.at[kind, me], d)

    def adapter_wait(kind, dst):
        loads[6 + kind].wait()

        def one(d):
            remote(
                pool_hbm.at[:, 1 + kind, :, pl.ds(0, 512)],
                dst.at[pl.ds(2 * d, 2)], ad_ss.at[kind, d], ad_rs.at[kind, d], d).wait_recv()
        peers(one)

    def spray(send, recv, ss, rs, per_peer):
        def one(d):
            src = send.at[d] if per_peer else send
            remote(src, recv.at[me], ss.at[d], rs.at[me], d).start()
        peers(one)

    def spray_wait(send, recv, ss, rs, per_peer):
        def one(d):
            src = send.at[d] if per_peer else send
            remote(src, recv.at[d], ss.at[d], rs.at[d], d).wait_recv()
        peers(one)

    def spray_drain(send, recv, ss, rs, per_peer):
        def one(d):
            src = send.at[d] if per_peer else send
            remote(src, recv.at[me], ss.at[d], rs.at[me], d).wait_send()
        peers(one)

    for j in range(CHUNKS):
        x_cur[j] = x0[j]
        ag_begin(j)
    peers(lambda d: adapter(0, bq, d).start())

    i, k = iota((256, 256), 0), iota((256, 256), 1)
    perm[...] = (k == ((i >> 2) & 15) * 16 + (i >> 6) * 4 + (i & 3)).astype(F32).astype(BF)
    perm_t[...] = (k == ((i >> 2) & 3) * 64 + (i >> 4) * 4 + (i & 3)).astype(F32).astype(BF)
    i, k = iota((512, 320), 0), iota((512, 320), 1)
    perm_q[...] = (k == ((i >> 2) & 7) * 64 + (i >> 5) * 4 + (i & 3)).astype(F32).astype(BF)
    qs_send[...] = jnp.zeros_like(qs_send)
    os_send[...] = jnp.zeros_like(os_send)
    kvbuf[pl.ds(KEYS, 256), :] = jnp.zeros((256, 256), BF)
    for part in range(4):
        keys = 384
        i, k = iota((256, keys), 0), iota((256, keys), 1)
        ok = ((i & 3) == part) & ((i >> 5) == (k & 7)) & ((k >> 3) < length_col[...])
        bias[:, pl.ds(part * keys, keys)] = jnp.where(ok, 0.0, -1e30)
    i, k = iota((256, 256), 0), iota((256, 256), 1)
    fresh = ((k & 15) == (i & 3)) & (((k >> 4) & 7) == (i >> 5))
    bias[:, pl.ds(KEYS, 256)] = jnp.where(fresh & (k < 128), 0.0, -1e30)

    for j in range(CHUNKS):
        ag_forward(j)
    peers(lambda d: adapter(1, ao, d).start())
    loads[0].wait()
    loads[3].wait()

    def step(s, carry):
        @pl.when(s == 1)
        def _():
            i, k = iota((256, 256), 0), iota((256, 256), 1)
            fresh = ((k & 15) == (i & 3)) & (((k >> 4) & 7) == (i >> 5))
            bias[:, pl.ds(KEYS, 256)] = jnp.where(fresh, 0.0, -1e30)
            for j in range(CHUNKS):
                ag_forward(j)

        squares = jnp.zeros((64, 1), F32)
        shrink = jnp.zeros((32, 64), F32)
        for j in range(CHUNKS):
            ag_finish(j)
            xp[j] = dot(perm[...], xs[j].reshape(256, LANES)).astype(BF)
            for q in range(4):
                x = xp[j, q * 64:(q + 1) * 64, :]
                wide = x.astype(F32)
                squares += jnp.sum(wide * wide, axis=1, keepdims=True)
                a = aq[:, :, q * QUARTER + j * LANES:q * QUARTER + (j + 1) * LANES].reshape(32, LANES)
                shrink += dot_nt(a, x)
        here = page_row[...] == 2 * me + (iota((32, 64), 0) >> 4)
        shrink = jnp.where(here, shrink, 0.0)
        qs_send[:, 0:64] = (shrink[0:16] + shrink[16:32]).astype(BF)
        qs_recv[me] = qs_send[...]
        spray(qs_send, qs_recv, qs_ss, qs_rs, False)
        scale = lax.rsqrt(squares * (1.0 / 8192.0) + norm_epsilon)

        @pl.when(s == 0)
        def _():
            loads[1].wait()
            loads[2].wait()

        def project(n, acc):
            j, q = n // 4, n % 4
            x = xp[j, pl.ds(pl.multiple_of(q * 64, 64), 64), :]
            at = pl.ds(pl.multiple_of(q * QUARTER + j * LANES, LANES), LANES)
            return acc[0] + dot(x, wq[at, :]), acc[1] + dot(x, wkv[at, :])
        query, keyval = lax.fori_loop(
            0, 4 * CHUNKS, project, (jnp.zeros((64, 512), F32), jnp.zeros((64, 128), F32)))
        tq[pl.ds(256, 64), :] = (keyval * scale).astype(BF)

        spread_of = (iota((16, 512), 1) & 15) == iota((16, 512), 0)
        spread_of = spread_of.astype(F32).astype(BF)
        page_hit = page_col[...] == (iota((64, 512), 1) >> 4)

        @pl.when(s == 0)
        def _():
            adapter_wait(0, bq)
        spray_wait(qs_send, qs_recv, qs_ss, qs_rs, False)
        qs = jnp.sum(qs_recv[...].astype(F32), axis=0)
        low = dot(qs.T[0:64].astype(BF), spread_of)
        low = jnp.where(page_hit, low, 0.0).astype(BF)
        query = ((query + dot(low, bq[...].reshape(512, 512))) * scale).astype(BF)
        for h in range(4):
            tq[pl.ds(h * 64, 64), :] = query[:, h * 128:(h + 1) * 128]
        q_send[...] = dot(perm_q[...], tq[...]).astype(BF).reshape(16, 32, 128)
        q_recv[me] = q_send[me]
        spray(q_send, q_recv, q_ss, q_rs, True)
        spray_wait(q_send, q_recv, q_ss, q_rs, True)

        cos, sin = cosine[s], sine[s]

        def turn(v, n):
            flat = v.astype(F32).reshape(n * 16, 128)
            swapped = pltpu.roll(flat, 64, 1)
            both = flat.reshape(n, 16, 128) * cos[None] + swapped.reshape(n, 16, 128) * sin[None]
            return both.reshape(n * 16, 128).astype(BF)
        queries = turn(q_recv[:, 0:16, :], 16)
        fresh_kv = q_recv[:, 16:32, :].reshape(8, 2, 16, 128)
        new_at = pl.ds(pl.multiple_of(KEYS + 128 * s, 128), 128)
        kvbuf[new_at, 0:128] = turn(fresh_kv[:, 0], 8)
        kvbuf[new_at, 128:256] = fresh_kv[:, 1].reshape(128, 128)
        for half in range(2):
            rows = slice(half * 128, half * 128 + 128)
            score = dot_nt(queries[rows], kvbuf[:, 0:128]) * (float(HD) ** -0.5) + bias[rows, :]
            power = jnp.exp(score - jnp.max(score, axis=1, keepdims=True))
            total = jnp.sum(power, axis=1, keepdims=True)
            mixed = dot(power.astype(BF), kvbuf[:, 128:256]) / total
            a_send[half * 8:half * 8 + 8] = mixed.astype(BF).reshape(8, 16, 128)
        a_recv[me] = a_send[me]
        spray(a_send, a_recv, a_ss, a_rs, True)

        @pl.when(s == 0)
        def _():
            adapter_wait(1, ao)
            loads[4].wait()
            loads[5].wait()
        spray_wait(a_send, a_recv, a_ss, a_rs, True)

        heads = dot(perm[...], a_recv[...].reshape(256, 128)).astype(BF)
        for h in range(4):
            am[:, h * 128:(h + 1) * 128] = heads[h * 64:(h + 1) * 64]
        shrunk = dot_nt(ao[...].reshape(512, 512), am[...])
        shrunk = jnp.where(page_row[...] == (iota((512, 64), 0) >> 4), shrunk, 0.0)
        os_send[:, 0:64] = jnp.sum(shrunk.reshape(32, 16, 64), axis=0).astype(BF)
        os_recv[me] = os_send[...]
        spray(os_send, os_recv, os_ss, os_rs, False)

        def low_out():
            spray_wait(os_send, os_recv, os_ss, os_rs, False)
            os = jnp.sum(os_recv[...].astype(F32), axis=0)
            own = dot(os.T[0:64].astype(BF), spread_of[:, 0:32])
            mine = page_col[...] == 2 * me + (iota((64, 32), 1) >> 4)
            return jnp.where(mine, own, 0.0).astype(BF)

        def rs1(j):
            return remote(bs.at[j, :, 1 - c], r1.at[j], rs1_ss.at[j], rs1_rs.at[j], c_peer)

        def rs2(j):
            return remote(s1.at[j, :, 1 - y], r2.at[j], rs2_ss.at[j], rs2_rs.at[j], y_peer)

        def rs3(j, dz):
            zz = lax.rem(z + dz, 4)
            return remote(s2.at[j, zz], r3.at[j, z], rs3_ss.at[j, dz], rs3_rs.at[j, z], zz * 4 + y * 2 + c)

        def rs3_wait(j, zz):
            remote(s2.at[j, zz], r3.at[j, zz], rs3_ss.at[j, 0], rs3_rs.at[j, zz], y_peer).wait_recv()

        for j in range(CHUNKS):
            ag_drain(j)
        own = low_out()
        for j in range(CHUNKS):
            def outward(q, carry):
                at = pl.ds(pl.multiple_of(q * QUARTER + j * LANES, LANES), LANES)
                piece = dot(am[...], wo[:, at]) + dot(own, bo[:, :, at].reshape(32, LANES))
                pb[pl.ds(pl.multiple_of(q * 64, 64), 64), :] = piece.astype(BF)
                return carry
            lax.fori_loop(0, 4, outward, 0)
            bs[j] = dot(perm_t[...], pb[...]).astype(BF).reshape(8, 2, 16, LANES)
            rs1(j).start()
        for j in range(CHUNKS):
            rs1(j).wait_recv()
            s1[j] = (bs[j, :, c].astype(F32) + r1[j].astype(F32)).astype(BF).reshape(4, 2, 16, LANES)
            rs2(j).start()
        for j in range(CHUNKS):
            rs2(j).wait_recv()
            s2[j] = (s1[j, :, y].astype(F32) + r2[j].astype(F32)).astype(BF)
            for dz in (1, 2, 3):
                rs3(j, dz).start()
        for j in range(CHUNKS):
            total = s2[j, z].astype(F32)
            for dz in (1, 2, 3):
                zz = lax.rem(z + dz, 4)
                rs3_wait(j, zz)
                total += r3[j, zz].astype(F32)
            update = total.astype(BF)
            out[s, j] = update
            x_cur[j] = (x_cur[j].astype(F32) + update.astype(F32)).astype(BF)

            @pl.when(s == 0)
            def _():
                ag_begin(j)
        for j in range(CHUNKS):
            rs1(j).wait_send()
            rs2(j).wait_send()
            for dz in (1, 2, 3):
                rs3(j, dz).wait_send()
        spray_drain(qs_send, qs_recv, qs_ss, qs_rs, False)
        spray_drain(q_send, q_recv, q_ss, q_rs, True)
        spray_drain(a_send, a_recv, a_ss, a_rs, True)
        spray_drain(os_send, os_recv, os_ss, os_rs, False)
        return carry

    lax.fori_loop(0, 2, step, 0)
    peers(lambda d: adapter(0, bq, d).wait_send())
    peers(lambda d: adapter(1, ao, d).wait_send())


def on_device_fused(
    hidden_state, query_weight, keyval_weight, output_weight, cache_entries, adapter_pool,
    page_table, fetch_list, row_tenant, cache_length,
):
    tenants = jnp.arange(page_table.shape[0], dtype=jnp.int32)
    row_page = jnp.sum(jnp.where(row_tenant[:, None] == tenants[None, :], page_table[None, :], 0), axis=1)
    x0 = hidden_state.reshape(OWN, 4, CHUNKS, LANES).transpose(2, 1, 0, 3).reshape(CHUNKS, 16, LANES)
    half = HD // 2
    frequency = rope_base ** (-2.0 * jnp.arange(half, dtype=F32) / HD)
    positions = cache_length[None, :] + jnp.arange(2, dtype=jnp.int32)[:, None]
    angles = positions.astype(F32)[:, :, None] * frequency[None, None, :]
    cos, sin = jnp.cos(angles), jnp.sin(angles)
    cosine = jnp.tile(jnp.concatenate([cos, cos], axis=-1), (1, 4, 1))
    sine = jnp.tile(jnp.concatenate([-sin, sin], axis=-1), (1, 4, 1))
    length_col = jnp.tile(cache_length, 64)[:, None]
    vmem = pl.BlockSpec(memory_space=pltpu.VMEM)
    anywhere = pl.BlockSpec(memory_space=pl.ANY)
    V = pltpu.VMEM
    D_ = pltpu.SemaphoreType.DMA
    result = pl.pallas_call(
        fused,
        out_shape=jax.ShapeDtypeStruct((2, CHUNKS, 16, LANES), BF),
        in_specs=[vmem] * 6 + [anywhere] * 5,
        out_specs=vmem,
        scratch_shapes=[
            V((8192, 512), BF), V((8192, 128), BF), V((512, 8192), BF),
            V((2, 16, 8192), BF), V((2, 16, 8192), BF), V((32, 16, 512), BF), V((32, 16, 512), BF),
            V((KEYS + 256, 256), BF), V((256, KEYS + 256), F32),
            V((256, 256), BF), V((256, 256), BF), V((512, 320), BF),
            V((CHUNKS, 16, LANES), BF), V((CHUNKS, 16, 16, LANES), BF), V((CHUNKS, 256, LANES), BF),
            V((256, LANES), BF), V((CHUNKS, 8, 2, 16, LANES), BF),
            V((CHUNKS, 8, 16, LANES), BF), V((CHUNKS, 4, 2, 16, LANES), BF),
            V((CHUNKS, 4, 16, LANES), BF), V((CHUNKS, 4, 16, LANES), BF), V((CHUNKS, 4, 16, LANES), BF),
            V((16, 128), BF), V((16, 16, 128), BF), V((320, 128), BF),
            V((16, 32, 128), BF), V((16, 32, 128), BF),
            V((16, 16, 128), BF), V((16, 16, 128), BF), V((64, 512), BF),
            V((16, 128), BF), V((16, 16, 128), BF),
            D_((8,)), D_((2, 16)), D_((2, 16)), D_((CHUNKS, 4)), D_((CHUNKS, 4)), D_((CHUNKS, 8)),
            D_((CHUNKS, 16)),
            D_((16,)), D_((16,)), D_((16,)), D_((16,)), D_((16,)), D_((16,)), D_((16,)), D_((16,)),
            D_((CHUNKS,)), D_((CHUNKS,)), D_((CHUNKS,)), D_((CHUNKS,)), D_((CHUNKS, 4)), D_((CHUNKS, 4)),
        ],
        compiler_params=pltpu.CompilerParams(
            collective_id=0, has_side_effects=True, vmem_limit_bytes=56 * 1024 * 1024),
    )(
        x0, row_page[:, None], row_page[None, :], length_col, cosine, sine,
        query_weight, keyval_weight, output_weight, cache_entries.reshape(KEYS, 2 * HD), adapter_pool,
    )
    result = result.reshape(2, CHUNKS, 4, OWN, LANES).transpose(0, 3, 2, 1, 4)
    return result.reshape(2, OWN, 4 * QUARTER)


def solution(mesh):
    local = on_device
    if mesh.shape["tensor"] == DEVS and mesh.shape["pool"] == 1:
        local = on_device_fused
    return jax.shard_map(
        local,
        mesh=mesh,
        in_specs=(
            P(("groups", "pool", "tensor"), None),
            P(None, "tensor"),
            P(None, "tensor"),
            P("tensor", None),
            P(("groups", "pool", "tensor"), None, None, None),
            P(("groups", "pool", "tensor"), None, None, None),
            P("groups"),
            P("groups"),
            P(("groups", "pool")),
            P(("groups", "pool", "tensor")),
        ),
        out_specs=P(None, ("groups", "pool", "tensor"), None),
        check_vma=False,
    )
```

```python
import math

import jax
import jax.numpy as jnp
from jax import lax
from jax.experimental import pallas as pl
from jax.experimental.pallas import tpu as pltpu
from jax.sharding import PartitionSpec as P

HEADS = 64
KVH = 8
HD = 128
FETCH = 32


rope_base = 500000.0
norm_epsilon = 1e-05


def rotate(vectors, positions):
    half_dim = vectors.shape[-1] // 2
    frequency = rope_base ** (-2.0 * jnp.arange(half_dim, dtype=jnp.float32) / vectors.shape[-1])
    angles = positions.astype(jnp.float32)[:, None] * frequency[None, :]
    cosine_term = jnp.cos(angles)[:, None, :]
    sine_term = jnp.sin(angles)[:, None, :]
    lead_half = vectors[..., :half_dim]
    trail_half = vectors[..., half_dim:]
    return jnp.concatenate(
        [
            lead_half * cosine_term - trail_half * sine_term,
            trail_half * cosine_term + lead_half * sine_term,
        ],
        axis=-1,
    )


def attend(query_rot, new_keys, new_values, cache_entries, cache_length):
    row_total = query_rot.shape[0]
    key_heads = cache_entries.shape[2]
    head_dim = query_rot.shape[2]
    group_size = query_rot.shape[1] // key_heads
    query_vectors = query_rot.reshape(row_total, key_heads, group_size, head_dim)
    cached_keys = cache_entries[..., :head_dim]
    cached_values = cache_entries[..., head_dim:]
    scale = float(head_dim) ** (-0.5)
    scores_cache = (
        jnp.einsum(
            "rhgd,rchd->rhgc", query_vectors, cached_keys, preferred_element_type=jnp.float32
        )
        * scale
    )
    in_length = jnp.arange(cache_entries.shape[1], dtype=jnp.int32)[None, :] < cache_length[:, None]
    scores_cache = jnp.where(in_length[:, None, None, :], scores_cache, -1e30)
    scores_new = (
        jnp.einsum("rhgd,rjhd->rhgj", query_vectors, new_keys, preferred_element_type=jnp.float32)
        * scale
    )
    highest = jnp.maximum(jnp.max(scores_cache, axis=-1), jnp.max(scores_new, axis=-1))[..., None]
    exp_cache = jnp.exp(scores_cache - highest)
    exp_new = jnp.exp(scores_new - highest)
    denominator = jnp.sum(exp_cache, axis=-1, keepdims=True) + jnp.sum(
        exp_new, axis=-1, keepdims=True
    )
    weight_cache = (exp_cache / denominator).astype(jnp.bfloat16)
    weight_new = (exp_new / denominator).astype(jnp.bfloat16)
    combined = jnp.einsum(
        "rhgc,rchd->rhgd", weight_cache, cached_values, preferred_element_type=jnp.float32
    )
    combined = combined + jnp.einsum(
        "rhgj,rjhd->rhgd", weight_new, new_values, preferred_element_type=jnp.float32
    )
    return combined.reshape(row_total, -1).astype(jnp.bfloat16)


def expand_matrix(shrink_matrix, selector_lowrank, up_adapter_tiles):
    spread = selector_lowrank[:, :, None] * shrink_matrix[:, None, :]
    return jnp.einsum("nfk,fkc->nc", spread, up_adapter_tiles, preferred_element_type=jnp.float32)


def on_device(
    hidden_state,
    query_weight,
    keyval_weight,
    output_weight,
    cache_entries,
    adapter_pool,
    page_table,
    fetch_list,
    row_tenant,
    cache_length,
):
    tensor_count = lax.axis_size("tensor")
    pool_count = lax.axis_size("pool")
    tensor_index = lax.axis_index("tensor")
    device_index = lax.axis_index("pool") * tensor_count + tensor_index
    row_count = hidden_state.shape[0]
    model_width = hidden_state.shape[1]
    block_width = model_width // tensor_count
    slot_count = adapter_pool.shape[0]
    owner_count = pool_count * tensor_count
    capacity = max(2, (FETCH + owner_count - 1) // owner_count)
    matched = fetch_list[:, None] == jnp.arange(page_table.shape[0], dtype=jnp.int32)[None, :]
    page_ids = jnp.sum(jnp.where(matched, page_table[None, :], 0), axis=1)
    owners = page_ids // slot_count
    slot_ids = page_ids % slot_count
    fetch_order = jnp.arange(FETCH, dtype=jnp.int32)
    earlier = (owners[:, None] == owners[None, :]) & (fetch_order[None, :] < fetch_order[:, None])
    owner_rank = jnp.sum(earlier.astype(jnp.int32), axis=1)
    owned_here = owners == device_index
    chosen = owned_here[None, :] & (
        owner_rank[None, :] == jnp.arange(capacity, dtype=jnp.int32)[:, None]
    )
    send_slots = jnp.sum(jnp.where(chosen, slot_ids[None, :], 0), axis=1)
    present = jnp.any(chosen, axis=1).astype(jnp.bfloat16)
    outgoing = jnp.take(adapter_pool, send_slots, axis=0) * present[:, None, None, None]
    doubled = jnp.concatenate([outgoing] * pool_count, axis=3)
    arrived = lax.all_to_all(doubled, ("pool", "tensor"), split_axis=3, concat_axis=0, tiled=True)
    adapter_tiles = jnp.take(arrived, owners * capacity + owner_rank, axis=0)
    down_query = adapter_tiles[:, 0]
    up_query = adapter_tiles[:, 1]
    down_out = adapter_tiles[:, 2]
    up_projected = adapter_tiles[:, 3]
    row_hits = row_tenant[:, None] == fetch_list[None, :]
    onehot_wide = row_hits.astype(jnp.float32)
    selector_lowrank = row_hits.astype(jnp.bfloat16)
    column_start = tensor_index * block_width
    query_cols = query_weight.shape[1]
    keyval_cols = keyval_weight.shape[1]
    residual = hidden_state
    new_keys = []
    new_values = []
    updates = []
    for step_index in range(2):
        widened = residual.astype(jnp.float32)
        normalized_input = (
            widened * lax.rsqrt(jnp.mean(widened * widened, axis=1, keepdims=True) + norm_epsilon)
        ).astype(jnp.bfloat16)
        features_part = lax.all_gather(normalized_input, "tensor", axis=0, tiled=True)
        query_baseline = jnp.dot(features_part, query_weight, preferred_element_type=jnp.float32)
        keyval = jnp.dot(features_part, keyval_weight, preferred_element_type=jnp.float32)
        own_cols = lax.dynamic_slice_in_dim(features_part, column_start, block_width, 1)
        per_tenant = jnp.einsum(
            "nd,fkd->nfk", own_cols, down_query, preferred_element_type=jnp.float32
        )
        shrink_matrix = jnp.sum(per_tenant * onehot_wide[:, :, None], axis=1)
        projected = jnp.concatenate([query_baseline, keyval, shrink_matrix], axis=1)
        shrink_query = lax.psum(projected[:, query_cols + keyval_cols :], "tensor").astype(
            jnp.bfloat16
        )
        query_vectors = (
            projected[:, :query_cols] + expand_matrix(shrink_query, selector_lowrank, up_query)
        ).astype(jnp.bfloat16)
        keyval = projected[:, query_cols : query_cols + keyval_cols].astype(jnp.bfloat16)
        query_rows, keyval_rows = (
            lax.all_to_all(query_vectors, "tensor", split_axis=0, concat_axis=1, tiled=True),
            lax.all_to_all(keyval, "tensor", split_axis=0, concat_axis=1, tiled=True),
        )
        positions = cache_length + step_index
        query_rot = rotate(
            query_rows.reshape(row_count, HEADS, HD).astype(jnp.float32), positions
        ).astype(jnp.bfloat16)
        keyval_rows = keyval_rows.reshape(row_count, KVH, 2 * HD)
        key_rot = rotate(keyval_rows[..., :HD].astype(jnp.float32), positions).astype(jnp.bfloat16)
        new_keys.append(key_rot)
        new_values.append(keyval_rows[..., HD:])
        attention_result = attend(
            query_rot,
            jnp.stack(new_keys, axis=1),
            jnp.stack(new_values, axis=1),
            cache_entries,
            cache_length,
        )
        head_rows = lax.all_to_all(
            attention_result, "tensor", split_axis=1, concat_axis=0, tiled=True
        )
        base_total = lax.psum_scatter(
            jnp.dot(head_rows, output_weight, preferred_element_type=jnp.float32),
            "tensor",
            scatter_dimension=0,
            tiled=True,
        )
        per_tenant = jnp.einsum(
            "nc,fkc->nfk", head_rows, down_out, preferred_element_type=jnp.float32
        )
        partial_out = jnp.sum(per_tenant * onehot_wide[:, :, None], axis=1)
        reduced_output = lax.psum(partial_out, "tensor").astype(jnp.bfloat16)
        adapter_columns = expand_matrix(reduced_output, selector_lowrank, up_projected)
        adapter_portion = lax.all_to_all(
            adapter_columns, "tensor", split_axis=0, concat_axis=1, tiled=True
        )
        state_update = (base_total + adapter_portion).astype(jnp.bfloat16)
        updates.append(state_update)
        residual = (residual.astype(jnp.float32) + state_update.astype(jnp.float32)).astype(
            jnp.bfloat16
        )
    return jnp.stack(updates)


DEVS = 16
OWN = 4
QUARTER = 2048
CHUNKS = 2
LANES = QUARTER // CHUNKS
KEYS = 1536
BF = jnp.bfloat16
F32 = jnp.float32


def iota(shape, dim):
    return lax.broadcasted_iota(jnp.int32, shape, dim)


def dot(a, b):
    return jnp.dot(a, b, preferred_element_type=F32)


def dot_nt(a, b):
    return lax.dot_general(a, b, (((1,), (1,)), ((), ())), preferred_element_type=F32)


def fused(
    x0, page_table, row_tenant, cache_length, wq_hbm, wkv_hbm, wo_hbm, cache_hbm, pool_hbm,
    out,
    wq, wkv, wo, aq, bo, bq, ao, kvbuf, bias, perm, perm_t, perm_q,
    page_col, page_row, cosine, sine, x_cur, xs, xp, pw, pb, bs, r1, s1, r2, s2, r3,
    qs_send, qs_recv, tq, q_send, q_recv, a_send, a_recv, am, os_send, os_recv,
    load_sem, ad_ss, ad_rs, agz_ss, agy_ss, agc_ss, ag_rs,
    qs_ss, qs_rs, q_ss, q_rs, a_ss, a_rs, os_ss, os_rs,
    rs1_ss, rs1_rs, rs2_ss, rs2_rs, rs3_ss, rs3_rs,
):
    me = lax.axis_index("tensor")
    z, y, c = me // 4, (me // 2) % 2, me % 2
    y_peer = z * 4 + (1 - y) * 2 + c
    c_peer = z * 4 + y * 2 + (1 - c)

    def remote(src, dst, ss, rs, peer):
        return pltpu.make_async_remote_copy(
            src_ref=src, dst_ref=dst, send_sem=ss, recv_sem=rs,
            device_id={"tensor": peer}, device_id_type=pl.DeviceIdType.MESH,
        )

    def peers(body):
        for i in range(1, DEVS):
            body(lax.rem(me + i, DEVS))

    loads = [
        pltpu.make_async_copy(pool_hbm.at[:, 0], aq, load_sem.at[0]),
        pltpu.make_async_copy(wq_hbm, wq, load_sem.at[1]),
        pltpu.make_async_copy(wkv_hbm, wkv, load_sem.at[2]),
        pltpu.make_async_copy(cache_hbm, kvbuf.at[pl.ds(0, KEYS)], load_sem.at[3]),
        pltpu.make_async_copy(wo_hbm, wo, load_sem.at[4]),
        pltpu.make_async_copy(pool_hbm.at[:, 3], bo, load_sem.at[5]),
        pltpu.make_async_copy(
            pool_hbm.at[:, 1, :, pl.ds(pl.multiple_of(me * 512, 512), 512)],
            bq.at[pl.ds(2 * me, 2)], load_sem.at[6]),
        pltpu.make_async_copy(
            pool_hbm.at[:, 2, :, pl.ds(pl.multiple_of(me * 512, 512), 512)],
            ao.at[pl.ds(2 * me, 2)], load_sem.at[7]),
    ]
    for load in loads:
        load.start()

    barrier = pltpu.get_barrier_semaphore()
    peers(lambda d: pl.semaphore_signal(
        barrier, inc=1, device_id={"tensor": d}, device_id_type=pl.DeviceIdType.MESH))
    pl.semaphore_wait(barrier, DEVS - 1)

    def ag_z(j, dz):
        zz = lax.rem(z + dz, 4)
        return remote(xs.at[j, me], xs.at[j, me], agz_ss.at[j, dz], ag_rs.at[j, me], zz * 4 + y * 2 + c)

    def ag_y(j, zz):
        b = zz * 4 + y * 2 + c
        return remote(xs.at[j, b], xs.at[j, b], agy_ss.at[j, zz], ag_rs.at[j, b], y_peer)

    def ag_c(j, zz, yy):
        b = zz * 4 + yy * 2 + c
        return remote(xs.at[j, b], xs.at[j, b], agc_ss.at[j, zz * 2 + yy], ag_rs.at[j, b], c_peer)

    def ag_wait(j, b):
        remote(xs.at[j, b], xs.at[j, b], agz_ss.at[j, 0], ag_rs.at[j, b], c_peer).wait_recv()

    def ag_begin(j):
        xs[j, me] = x_cur[j]
        for dz in (1, 2, 3):
            ag_z(j, dz).start()
        ag_y(j, z).start()
        ag_c(j, z, y).start()

    def ag_forward(j):
        for dz in (1, 2, 3):
            zz = lax.rem(z + dz, 4)
            ag_wait(j, zz * 4 + y * 2 + c)
            ag_y(j, zz).start()
            ag_c(j, zz, y).start()

    def ag_cross(j):
        for dz in range(4):
            zz = lax.rem(z + dz, 4)
            ag_wait(j, zz * 4 + (1 - y) * 2 + c)
            ag_c(j, zz, 1 - y).start()

    def ag_finish(j):
        for b in range(8):
            ag_wait(j, b * 2 + (1 - c))

    def ag_drain(j):
        for dz in (1, 2, 3):
            ag_z(j, dz).wait_send()
        for zz in range(4):
            ag_y(j, zz).wait_send()
            for yy in range(2):
                ag_c(j, zz, yy).wait_send()

    def adapter(kind, dst, d):
        return remote(
            pool_hbm.at[:, 1 + kind, :, pl.ds(pl.multiple_of(d * 512, 512), 512)],
            dst.at[pl.ds(2 * me, 2)], ad_ss.at[kind, d], ad_rs.at[kind, me], d)

    def adapter_wait(kind, dst):
        loads[6 + kind].wait()

        def one(d):
            remote(
                pool_hbm.at[:, 1 + kind, :, pl.ds(0, 512)],
                dst.at[pl.ds(2 * d, 2)], ad_ss.at[kind, d], ad_rs.at[kind, d], d).wait_recv()
        peers(one)

    def spray(send, recv, ss, rs, per_peer):
        def one(d):
            src = send.at[d] if per_peer else send
            remote(src, recv.at[me], ss.at[d], rs.at[me], d).start()
        peers(one)

    def spray_wait(send, recv, ss, rs, per_peer):
        def one(d):
            src = send.at[d] if per_peer else send
            remote(src, recv.at[d], ss.at[d], rs.at[d], d).wait_recv()
        peers(one)

    def spray_drain(send, recv, ss, rs, per_peer):
        def one(d):
            src = send.at[d] if per_peer else send
            remote(src, recv.at[me], ss.at[d], rs.at[me], d).wait_send()
        peers(one)

    for j in range(CHUNKS):
        x_cur[j] = jnp.concatenate(
            [x0[:, q * QUARTER + j * LANES:q * QUARTER + (j + 1) * LANES].astype(F32) for q in range(4)],
            axis=0).astype(BF)
        ag_begin(j)
    peers(lambda d: adapter(0, bq, d).start())
    peers(lambda d: adapter(1, ao, d).start())

    col, line = jnp.zeros((64, 128), jnp.int32), jnp.zeros((8, 64), jnp.int32)
    for r in range(64):
        page = page_table[row_tenant[r]]
        col = jnp.where(iota((64, 128), 0) == r, page, col)
        line = jnp.where(iota((8, 64), 1) == r, page, line)
    for n in range(4):
        page_col[:, n * 128:(n + 1) * 128] = col
    page_row[...] = line

    def by_row(shape):
        got = jnp.zeros(shape, jnp.int32)
        for r in range(OWN):
            got = jnp.where((iota(shape, 0) & 3) == r, cache_length[r], got)
        return got
    lane = iota((16, 128), 1)
    frequency = jnp.exp((lane & 63).astype(F32) * (-2.0 / HD * math.log(rope_base)))
    for n in range(2):
        angle = (by_row((16, 128)) + n).astype(F32) * frequency
        cosine[n] = jnp.cos(angle)
        turned = jnp.sin(angle)
        sine[n] = jnp.where(lane < 64, -turned, turned)

    i, k = iota((256, 256), 0), iota((256, 256), 1)
    perm[...] = (k == ((i >> 2) & 15) * 16 + (i >> 6) * 4 + (i & 3)).astype(F32).astype(BF)
    perm_t[...] = (k == ((i >> 2) & 3) * 64 + (i >> 4) * 4 + (i & 3)).astype(F32).astype(BF)
    i, k = iota((512, 320), 0), iota((512, 320), 1)
    perm_q[...] = (k == ((i >> 2) & 7) * 64 + (i >> 5) * 4 + (i & 3)).astype(F32).astype(BF)
    qs_send[...] = jnp.zeros_like(qs_send)
    os_send[...] = jnp.zeros_like(os_send)
    kvbuf[pl.ds(KEYS, 256), :] = jnp.zeros((256, 256), BF)
    for part in range(4):
        keys = 384
        i, k = iota((256, keys), 0), iota((256, keys), 1)
        ok = ((i & 3) == part) & ((i >> 5) == (k & 7)) & ((k >> 3) < by_row((256, keys)))
        bias[:, pl.ds(part * keys, keys)] = jnp.where(ok, 0.0, -1e30)
    i, k = iota((256, 256), 0), iota((256, 256), 1)
    fresh = ((k & 15) == (i & 3)) & (((k >> 4) & 7) == (i >> 5))
    bias[:, pl.ds(KEYS, 256)] = jnp.where(fresh & (k < 128), 0.0, -1e30)

    for j in range(CHUNKS):
        ag_forward(j)
    for j in range(CHUNKS):
        ag_cross(j)
    loads[0].wait()
    loads[3].wait()

    def step(s, carry):
        @pl.when(s == 1)
        def _():
            i, k = iota((256, 256), 0), iota((256, 256), 1)
            fresh = ((k & 15) == (i & 3)) & (((k >> 4) & 7) == (i >> 5))
            bias[:, pl.ds(KEYS, 256)] = jnp.where(fresh, 0.0, -1e30)
            for j in range(CHUNKS):
                ag_forward(j)
            for j in range(CHUNKS):
                ag_cross(j)

        squares = jnp.zeros((64, 1), F32)
        shrink = jnp.zeros((32, 64), F32)
        for j in range(CHUNKS):
            ag_finish(j)
            xp[j] = dot(perm[...], xs[j].reshape(256, LANES)).astype(BF)
            for q in range(4):
                x = xp[j, q * 64:(q + 1) * 64, :]
                wide = x.astype(F32)
                squares += jnp.sum(wide * wide, axis=1, keepdims=True)
                a = aq[:, :, q * QUARTER + j * LANES:q * QUARTER + (j + 1) * LANES].reshape(32, LANES)
                shrink += dot_nt(a, x)
        here = page_row[0:1, :] == 2 * me + (iota((32, 64), 0) >> 4)
        shrink = jnp.where(here, shrink, 0.0)
        qs_send[:, 0:64] = (shrink[0:16] + shrink[16:32]).astype(BF)
        qs_recv[me] = qs_send[...]
        spray(qs_send, qs_recv, qs_ss, qs_rs, False)
        scale = lax.rsqrt(squares * (1.0 / 8192.0) + norm_epsilon)

        @pl.when(s == 0)
        def _():
            loads[1].wait()
            loads[2].wait()

        def project(n, acc):
            j, q = n // 4, n % 4
            x = xp[j, pl.ds(pl.multiple_of(q * 64, 64), 64), :]
            at = pl.ds(pl.multiple_of(q * QUARTER + j * LANES, LANES), LANES)
            return acc[0] + dot(x, wq[at, :]), acc[1] + dot(x, wkv[at, :])
        query, keyval = lax.fori_loop(
            0, 4 * CHUNKS, project, (jnp.zeros((64, 512), F32), jnp.zeros((64, 128), F32)))
        tq[pl.ds(256, 64), :] = (keyval * scale).astype(BF)

        spread_of = (iota((16, 512), 1) & 15) == iota((16, 512), 0)
        spread_of = spread_of.astype(F32).astype(BF)
        page_hit = page_col[...] == (iota((64, 512), 1) >> 4)

        @pl.when(s == 0)
        def _():
            adapter_wait(0, bq)
        spray_wait(qs_send, qs_recv, qs_ss, qs_rs, False)
        qs = jnp.sum(qs_recv[...].astype(F32), axis=0)
        low = dot(qs.T[0:64].astype(BF), spread_of)
        low = jnp.where(page_hit, low, 0.0).astype(BF)
        query = ((query + dot(low, bq[...].reshape(512, 512))) * scale).astype(BF)
        for h in range(4):
            tq[pl.ds(h * 64, 64), :] = query[:, h * 128:(h + 1) * 128]
        q_send[...] = dot(perm_q[...], tq[...]).astype(BF).reshape(16, 32, 128)
        q_recv[me] = q_send[me]
        spray(q_send, q_recv, q_ss, q_rs, True)
        spray_wait(q_send, q_recv, q_ss, q_rs, True)

        cos, sin = cosine[s], sine[s]

        def turn(v, n):
            flat = v.astype(F32).reshape(n * 16, 128)
            swapped = pltpu.roll(flat, 64, 1)
            both = flat.reshape(n, 16, 128) * cos[None] + swapped.reshape(n, 16, 128) * sin[None]
            return both.reshape(n * 16, 128).astype(BF)
        queries = turn(q_recv[:, 0:16, :], 16)
        fresh_kv = q_recv[:, 16:32, :].reshape(8, 2, 16, 128)
        new_at = pl.ds(pl.multiple_of(KEYS + 128 * s, 128), 128)
        kvbuf[new_at, 0:128] = turn(fresh_kv[:, 0], 8)
        kvbuf[new_at, 128:256] = fresh_kv[:, 1].reshape(128, 128)
        for half in range(2):
            rows = slice(half * 128, half * 128 + 128)
            score = dot_nt(queries[rows], kvbuf[:, 0:128]) * (float(HD) ** -0.5) + bias[rows, :]
            power = jnp.exp(score - jnp.max(score, axis=1, keepdims=True))
            total = jnp.sum(power, axis=1, keepdims=True)
            mixed = dot(power.astype(BF), kvbuf[:, 128:256]) / total
            a_send[half * 8:half * 8 + 8] = mixed.astype(BF).reshape(8, 16, 128)
        a_recv[me] = a_send[me]
        spray(a_send, a_recv, a_ss, a_rs, True)

        @pl.when(s == 0)
        def _():
            adapter_wait(1, ao)
            loads[4].wait()
            loads[5].wait()
        spray_wait(a_send, a_recv, a_ss, a_rs, True)

        heads = dot(perm[...], a_recv[...].reshape(256, 128)).astype(BF)
        for h in range(4):
            am[:, h * 128:(h + 1) * 128] = heads[h * 64:(h + 1) * 64]
        shrunk = dot_nt(ao[...].reshape(512, 512), am[...])
        shrunk = jnp.where(page_row[0:1, :] == (iota((512, 64), 0) >> 4), shrunk, 0.0)
        os_send[:, 0:64] = jnp.sum(shrunk.reshape(32, 16, 64), axis=0).astype(BF)
        os_recv[me] = os_send[...]
        spray(os_send, os_recv, os_ss, os_rs, False)

        def low_out():
            spray_wait(os_send, os_recv, os_ss, os_rs, False)
            os = jnp.sum(os_recv[...].astype(F32), axis=0)
            own = dot(os.T[0:64].astype(BF), spread_of[:, 0:32])
            mine = page_col[:, 0:32] == 2 * me + (iota((64, 32), 1) >> 4)
            return jnp.where(mine, own, 0.0).astype(BF)

        def rs1(j):
            return remote(bs.at[j, :, 1 - c], r1.at[j], rs1_ss.at[j], rs1_rs.at[j], c_peer)

        def rs2(j):
            return remote(s1.at[j, :, 1 - y], r2.at[j], rs2_ss.at[j], rs2_rs.at[j], y_peer)

        def rs3(j, dz):
            zz = lax.rem(z + dz, 4)
            return remote(s2.at[j, zz], r3.at[j, z], rs3_ss.at[j, dz], rs3_rs.at[j, z], zz * 4 + y * 2 + c)

        def rs3_wait(j, zz):
            remote(s2.at[j, zz], r3.at[j, zz], rs3_ss.at[j, 0], rs3_rs.at[j, zz], y_peer).wait_recv()

        for j in range(CHUNKS):
            ag_drain(j)
        def outward(n, carry):
            j, q = n // 4, n % 4
            at = pl.ds(pl.multiple_of(q * QUARTER + j * LANES, LANES), LANES)
            pw[pl.ds(pl.multiple_of(n * 64, 64), 64), :] = dot(am[...], wo[:, at])
            return carry
        lax.fori_loop(0, 4 * CHUNKS, outward, 0)
        own = low_out()
        for j in range(CHUNKS):
            for q in range(4):
                n = j * 4 + q
                at = slice(q * QUARTER + j * LANES, q * QUARTER + (j + 1) * LANES)
                piece = pw[n * 64:(n + 1) * 64, :] + dot(own, bo[:, :, at].reshape(32, LANES))
                pb[q * 64:(q + 1) * 64, :] = piece.astype(BF)
            bs[j] = dot(perm_t[...], pb[...]).astype(BF).reshape(8, 2, 16, LANES)
            rs1(j).start()
        for j in range(CHUNKS):
            rs1(j).wait_recv()
            s1[j] = (bs[j, :, c].astype(F32) + r1[j].astype(F32)).astype(BF).reshape(4, 2, 16, LANES)
            rs2(j).start()
        for j in range(CHUNKS):
            rs2(j).wait_recv()
            s2[j] = (s1[j, :, y].astype(F32) + r2[j].astype(F32)).astype(BF)
            for dz in (1, 2, 3):
                rs3(j, dz).start()
        for j in range(CHUNKS):
            total = s2[j, z].astype(F32)
            for dz in (1, 2, 3):
                zz = lax.rem(z + dz, 4)
                rs3_wait(j, zz)
                total += r3[j, zz].astype(F32)
            update = total.astype(BF)
            out[s, j] = update
            x_cur[j] = (x_cur[j].astype(F32) + update.astype(F32)).astype(BF)

            @pl.when(s == 0)
            def _():
                ag_begin(j)
        for j in range(CHUNKS):
            rs1(j).wait_send()
            rs2(j).wait_send()
            for dz in (1, 2, 3):
                rs3(j, dz).wait_send()
        spray_drain(qs_send, qs_recv, qs_ss, qs_rs, False)
        spray_drain(q_send, q_recv, q_ss, q_rs, True)
        spray_drain(a_send, a_recv, a_ss, a_rs, True)
        spray_drain(os_send, os_recv, os_ss, os_rs, False)
        return carry

    lax.fori_loop(0, 2, step, 0)
    peers(lambda d: adapter(0, bq, d).wait_send())
    peers(lambda d: adapter(1, ao, d).wait_send())


def on_device_fused(
    hidden_state, query_weight, keyval_weight, output_weight, cache_entries, adapter_pool,
    page_table, fetch_list, row_tenant, cache_length,
):
    vmem = pl.BlockSpec(memory_space=pltpu.VMEM)
    scalars = pl.BlockSpec(memory_space=pltpu.SMEM)
    anywhere = pl.BlockSpec(memory_space=pl.ANY)
    V = pltpu.VMEM
    D_ = pltpu.SemaphoreType.DMA
    result = pl.pallas_call(
        fused,
        out_shape=jax.ShapeDtypeStruct((2, CHUNKS, 16, LANES), BF),
        in_specs=[vmem] + [scalars] * 3 + [anywhere] * 5,
        out_specs=vmem,
        scratch_shapes=[
            V((8192, 512), BF), V((8192, 128), BF), V((512, 8192), BF),
            V((2, 16, 8192), BF), V((2, 16, 8192), BF), V((32, 16, 512), BF), V((32, 16, 512), BF),
            V((KEYS + 256, 256), BF), V((256, KEYS + 256), F32),
            V((256, 256), BF), V((256, 256), BF), V((512, 320), BF),
            V((64, 512), jnp.int32), V((8, 64), jnp.int32), V((2, 16, 128), F32), V((2, 16, 128), F32),
            V((CHUNKS, 16, LANES), BF), V((CHUNKS, 16, 16, LANES), BF), V((CHUNKS, 256, LANES), BF),
            V((CHUNKS * 256, LANES), F32), V((256, LANES), BF), V((CHUNKS, 8, 2, 16, LANES), BF),
            V((CHUNKS, 8, 16, LANES), BF), V((CHUNKS, 4, 2, 16, LANES), BF),
            V((CHUNKS, 4, 16, LANES), BF), V((CHUNKS, 4, 16, LANES), BF), V((CHUNKS, 4, 16, LANES), BF),
            V((16, 128), BF), V((16, 16, 128), BF), V((320, 128), BF),
            V((16, 32, 128), BF), V((16, 32, 128), BF),
            V((16, 16, 128), BF), V((16, 16, 128), BF), V((64, 512), BF),
            V((16, 128), BF), V((16, 16, 128), BF),
            D_((8,)), D_((2, 16)), D_((2, 16)), D_((CHUNKS, 4)), D_((CHUNKS, 4)), D_((CHUNKS, 8)),
            D_((CHUNKS, 16)),
            D_((16,)), D_((16,)), D_((16,)), D_((16,)), D_((16,)), D_((16,)), D_((16,)), D_((16,)),
            D_((CHUNKS,)), D_((CHUNKS,)), D_((CHUNKS,)), D_((CHUNKS,)), D_((CHUNKS, 4)), D_((CHUNKS, 4)),
        ],
        compiler_params=pltpu.CompilerParams(
            collective_id=0, has_side_effects=True, vmem_limit_bytes=56 * 1024 * 1024),
    )(
        hidden_state, page_table, row_tenant, cache_length,
        query_weight, keyval_weight, output_weight, cache_entries.reshape(KEYS, 2 * HD), adapter_pool,
    )
    result = result.reshape(2, CHUNKS, 4, OWN, LANES).transpose(0, 3, 2, 1, 4)
    return result.reshape(2, OWN, 4 * QUARTER)


def solution(mesh):
    local = on_device
    if mesh.shape["tensor"] == DEVS and mesh.shape["pool"] == 1:
        local = on_device_fused
    return jax.shard_map(
        local,
        mesh=mesh,
        in_specs=(
            P(("groups", "pool", "tensor"), None),
            P(None, "tensor"),
            P(None, "tensor"),
            P("tensor", None),
            P(("groups", "pool", "tensor"), None, None, None),
            P(("groups", "pool", "tensor"), None, None, None),
            P("groups"),
            P("groups"),
            P(("groups", "pool")),
            P(("groups", "pool", "tensor")),
        ),
        out_specs=P(None, ("groups", "pool", "tensor"), None),
        check_vma=False,
    )
```

```python
import math

import jax
import jax.numpy as jnp
from jax import lax
from jax.experimental import pallas as pl
from jax.experimental.pallas import tpu as pltpu
from jax.sharding import PartitionSpec as P

HEADS = 64
KVH = 8
HD = 128
FETCH = 32


rope_base = 500000.0
norm_epsilon = 1e-05


def rotate(vectors, positions):
    half_dim = vectors.shape[-1] // 2
    frequency = rope_base ** (-2.0 * jnp.arange(half_dim, dtype=jnp.float32) / vectors.shape[-1])
    angles = positions.astype(jnp.float32)[:, None] * frequency[None, :]
    cosine_term = jnp.cos(angles)[:, None, :]
    sine_term = jnp.sin(angles)[:, None, :]
    lead_half = vectors[..., :half_dim]
    trail_half = vectors[..., half_dim:]
    return jnp.concatenate(
        [
            lead_half * cosine_term - trail_half * sine_term,
            trail_half * cosine_term + lead_half * sine_term,
        ],
        axis=-1,
    )


def attend(query_rot, new_keys, new_values, cache_entries, cache_length):
    row_total = query_rot.shape[0]
    key_heads = cache_entries.shape[2]
    head_dim = query_rot.shape[2]
    group_size = query_rot.shape[1] // key_heads
    query_vectors = query_rot.reshape(row_total, key_heads, group_size, head_dim)
    cached_keys = cache_entries[..., :head_dim]
    cached_values = cache_entries[..., head_dim:]
    scale = float(head_dim) ** (-0.5)
    scores_cache = (
        jnp.einsum(
            "rhgd,rchd->rhgc", query_vectors, cached_keys, preferred_element_type=jnp.float32
        )
        * scale
    )
    in_length = jnp.arange(cache_entries.shape[1], dtype=jnp.int32)[None, :] < cache_length[:, None]
    scores_cache = jnp.where(in_length[:, None, None, :], scores_cache, -1e30)
    scores_new = (
        jnp.einsum("rhgd,rjhd->rhgj", query_vectors, new_keys, preferred_element_type=jnp.float32)
        * scale
    )
    highest = jnp.maximum(jnp.max(scores_cache, axis=-1), jnp.max(scores_new, axis=-1))[..., None]
    exp_cache = jnp.exp(scores_cache - highest)
    exp_new = jnp.exp(scores_new - highest)
    denominator = jnp.sum(exp_cache, axis=-1, keepdims=True) + jnp.sum(
        exp_new, axis=-1, keepdims=True
    )
    weight_cache = (exp_cache / denominator).astype(jnp.bfloat16)
    weight_new = (exp_new / denominator).astype(jnp.bfloat16)
    combined = jnp.einsum(
        "rhgc,rchd->rhgd", weight_cache, cached_values, preferred_element_type=jnp.float32
    )
    combined = combined + jnp.einsum(
        "rhgj,rjhd->rhgd", weight_new, new_values, preferred_element_type=jnp.float32
    )
    return combined.reshape(row_total, -1).astype(jnp.bfloat16)


def expand_matrix(shrink_matrix, selector_lowrank, up_adapter_tiles):
    spread = selector_lowrank[:, :, None] * shrink_matrix[:, None, :]
    return jnp.einsum("nfk,fkc->nc", spread, up_adapter_tiles, preferred_element_type=jnp.float32)


def on_device(
    hidden_state,
    query_weight,
    keyval_weight,
    output_weight,
    cache_entries,
    adapter_pool,
    page_table,
    fetch_list,
    row_tenant,
    cache_length,
):
    tensor_count = lax.axis_size("tensor")
    pool_count = lax.axis_size("pool")
    tensor_index = lax.axis_index("tensor")
    device_index = lax.axis_index("pool") * tensor_count + tensor_index
    row_count = hidden_state.shape[0]
    model_width = hidden_state.shape[1]
    block_width = model_width // tensor_count
    slot_count = adapter_pool.shape[0]
    owner_count = pool_count * tensor_count
    capacity = max(2, (FETCH + owner_count - 1) // owner_count)
    matched = fetch_list[:, None] == jnp.arange(page_table.shape[0], dtype=jnp.int32)[None, :]
    page_ids = jnp.sum(jnp.where(matched, page_table[None, :], 0), axis=1)
    owners = page_ids // slot_count
    slot_ids = page_ids % slot_count
    fetch_order = jnp.arange(FETCH, dtype=jnp.int32)
    earlier = (owners[:, None] == owners[None, :]) & (fetch_order[None, :] < fetch_order[:, None])
    owner_rank = jnp.sum(earlier.astype(jnp.int32), axis=1)
    owned_here = owners == device_index
    chosen = owned_here[None, :] & (
        owner_rank[None, :] == jnp.arange(capacity, dtype=jnp.int32)[:, None]
    )
    send_slots = jnp.sum(jnp.where(chosen, slot_ids[None, :], 0), axis=1)
    present = jnp.any(chosen, axis=1).astype(jnp.bfloat16)
    outgoing = jnp.take(adapter_pool, send_slots, axis=0) * present[:, None, None, None]
    doubled = jnp.concatenate([outgoing] * pool_count, axis=3)
    arrived = lax.all_to_all(doubled, ("pool", "tensor"), split_axis=3, concat_axis=0, tiled=True)
    adapter_tiles = jnp.take(arrived, owners * capacity + owner_rank, axis=0)
    down_query = adapter_tiles[:, 0]
    up_query = adapter_tiles[:, 1]
    down_out = adapter_tiles[:, 2]
    up_projected = adapter_tiles[:, 3]
    row_hits = row_tenant[:, None] == fetch_list[None, :]
    onehot_wide = row_hits.astype(jnp.float32)
    selector_lowrank = row_hits.astype(jnp.bfloat16)
    column_start = tensor_index * block_width
    query_cols = query_weight.shape[1]
    keyval_cols = keyval_weight.shape[1]
    residual = hidden_state
    new_keys = []
    new_values = []
    updates = []
    for step_index in range(2):
        widened = residual.astype(jnp.float32)
        normalized_input = (
            widened * lax.rsqrt(jnp.mean(widened * widened, axis=1, keepdims=True) + norm_epsilon)
        ).astype(jnp.bfloat16)
        features_part = lax.all_gather(normalized_input, "tensor", axis=0, tiled=True)
        query_baseline = jnp.dot(features_part, query_weight, preferred_element_type=jnp.float32)
        keyval = jnp.dot(features_part, keyval_weight, preferred_element_type=jnp.float32)
        own_cols = lax.dynamic_slice_in_dim(features_part, column_start, block_width, 1)
        per_tenant = jnp.einsum(
            "nd,fkd->nfk", own_cols, down_query, preferred_element_type=jnp.float32
        )
        shrink_matrix = jnp.sum(per_tenant * onehot_wide[:, :, None], axis=1)
        projected = jnp.concatenate([query_baseline, keyval, shrink_matrix], axis=1)
        shrink_query = lax.psum(projected[:, query_cols + keyval_cols :], "tensor").astype(
            jnp.bfloat16
        )
        query_vectors = (
            projected[:, :query_cols] + expand_matrix(shrink_query, selector_lowrank, up_query)
        ).astype(jnp.bfloat16)
        keyval = projected[:, query_cols : query_cols + keyval_cols].astype(jnp.bfloat16)
        query_rows, keyval_rows = (
            lax.all_to_all(query_vectors, "tensor", split_axis=0, concat_axis=1, tiled=True),
            lax.all_to_all(keyval, "tensor", split_axis=0, concat_axis=1, tiled=True),
        )
        positions = cache_length + step_index
        query_rot = rotate(
            query_rows.reshape(row_count, HEADS, HD).astype(jnp.float32), positions
        ).astype(jnp.bfloat16)
        keyval_rows = keyval_rows.reshape(row_count, KVH, 2 * HD)
        key_rot = rotate(keyval_rows[..., :HD].astype(jnp.float32), positions).astype(jnp.bfloat16)
        new_keys.append(key_rot)
        new_values.append(keyval_rows[..., HD:])
        attention_result = attend(
            query_rot,
            jnp.stack(new_keys, axis=1),
            jnp.stack(new_values, axis=1),
            cache_entries,
            cache_length,
        )
        head_rows = lax.all_to_all(
            attention_result, "tensor", split_axis=1, concat_axis=0, tiled=True
        )
        base_total = lax.psum_scatter(
            jnp.dot(head_rows, output_weight, preferred_element_type=jnp.float32),
            "tensor",
            scatter_dimension=0,
            tiled=True,
        )
        per_tenant = jnp.einsum(
            "nc,fkc->nfk", head_rows, down_out, preferred_element_type=jnp.float32
        )
        partial_out = jnp.sum(per_tenant * onehot_wide[:, :, None], axis=1)
        reduced_output = lax.psum(partial_out, "tensor").astype(jnp.bfloat16)
        adapter_columns = expand_matrix(reduced_output, selector_lowrank, up_projected)
        adapter_portion = lax.all_to_all(
            adapter_columns, "tensor", split_axis=0, concat_axis=1, tiled=True
        )
        state_update = (base_total + adapter_portion).astype(jnp.bfloat16)
        updates.append(state_update)
        residual = (residual.astype(jnp.float32) + state_update.astype(jnp.float32)).astype(
            jnp.bfloat16
        )
    return jnp.stack(updates)


DEVS = 16
OWN = 4
QUARTER = 2048
CHUNKS = 2
LANES = QUARTER // CHUNKS
KEYS = 1536
BF = jnp.bfloat16
F32 = jnp.float32


def iota(shape, dim):
    return lax.broadcasted_iota(jnp.int32, shape, dim)


def dot(a, b):
    return jnp.dot(a, b, preferred_element_type=F32)


def dot_nt(a, b):
    return lax.dot_general(a, b, (((1,), (1,)), ((), ())), preferred_element_type=F32)


def fused(
    x0, page_table, row_tenant, cache_length, wq_hbm, wkv_hbm, wo_hbm, cache_hbm, pool_hbm,
    out,
    wq, wkv, wo, aq, bo, bq, ao, kvbuf, bias, perm, perm_t, perm_q,
    page_col, page_row, cosine, sine, x_cur, xs, xp, pw, pb, bs, r1, s1, r2, s2, r3,
    qs_send, qs_recv, tq, q_send, q_recv, a_send, a_recv, am, os_send, os_recv,
    load_sem, ad_ss, ad_rs, agz_ss, agy_ss, agc_ss, ag_rs,
    qs_ss, qs_rs, q_ss, q_rs, a_ss, a_rs, os_ss, os_rs,
    rs1_ss, rs1_rs, rs2_ss, rs2_rs, rs3_ss, rs3_rs,
):
    me = lax.axis_index("tensor")
    z, y, c = me // 4, (me // 2) % 2, me % 2
    y_peer = z * 4 + (1 - y) * 2 + c
    c_peer = z * 4 + y * 2 + (1 - c)

    def remote(src, dst, ss, rs, peer):
        return pltpu.make_async_remote_copy(
            src_ref=src, dst_ref=dst, send_sem=ss, recv_sem=rs,
            device_id={"tensor": peer}, device_id_type=pl.DeviceIdType.MESH,
        )

    def peers(body):
        for i in range(1, DEVS):
            body(lax.rem(me + i, DEVS))

    loads = [
        pltpu.make_async_copy(pool_hbm.at[:, 0], aq, load_sem.at[0]),
        pltpu.make_async_copy(wq_hbm, wq, load_sem.at[1]),
        pltpu.make_async_copy(wkv_hbm, wkv, load_sem.at[2]),
        pltpu.make_async_copy(cache_hbm, kvbuf.at[pl.ds(0, KEYS)], load_sem.at[3]),
        pltpu.make_async_copy(wo_hbm, wo, load_sem.at[4]),
        pltpu.make_async_copy(pool_hbm.at[:, 3], bo, load_sem.at[5]),
        pltpu.make_async_copy(
            pool_hbm.at[:, 1, :, pl.ds(pl.multiple_of(me * 512, 512), 512)],
            bq.at[pl.ds(2 * me, 2)], load_sem.at[6]),
        pltpu.make_async_copy(
            pool_hbm.at[:, 2, :, pl.ds(pl.multiple_of(me * 512, 512), 512)],
            ao.at[pl.ds(2 * me, 2)], load_sem.at[7]),
    ]
    for load in loads:
        load.start()

    barrier = pltpu.get_barrier_semaphore()
    peers(lambda d: pl.semaphore_signal(
        barrier, inc=1, device_id={"tensor": d}, device_id_type=pl.DeviceIdType.MESH))
    pl.semaphore_wait(barrier, DEVS - 1)

    def ag_z(j, dz):
        zz = lax.rem(z + dz, 4)
        return remote(xs.at[j, me], xs.at[j, me], agz_ss.at[j, dz], ag_rs.at[j, me], zz * 4 + y * 2 + c)

    def ag_y(j, zz):
        b = zz * 4 + y * 2 + c
        return remote(xs.at[j, b], xs.at[j, b], agy_ss.at[j, zz], ag_rs.at[j, b], y_peer)

    def ag_c(j, zz, yy):
        b = zz * 4 + yy * 2 + c
        return remote(xs.at[j, b], xs.at[j, b], agc_ss.at[j, zz * 2 + yy], ag_rs.at[j, b], c_peer)

    def ag_wait(j, b):
        remote(xs.at[j, b], xs.at[j, b], agz_ss.at[j, 0], ag_rs.at[j, b], c_peer).wait_recv()

    def ag_begin(j):
        xs[j, me] = x_cur[j]
        for dz in (1, 2, 3):
            ag_z(j, dz).start()
        ag_y(j, z).start()
        ag_c(j, z, y).start()

    def ag_forward(j):
        for dz in (1, 2, 3):
            zz = lax.rem(z + dz, 4)
            ag_wait(j, zz * 4 + y * 2 + c)
            ag_y(j, zz).start()
            ag_c(j, zz, y).start()

    def ag_cross(j):
        for dz in range(4):
            zz = lax.rem(z + dz, 4)
            ag_wait(j, zz * 4 + (1 - y) * 2 + c)
            ag_c(j, zz, 1 - y).start()

    def ag_finish(j):
        for b in range(8):
            ag_wait(j, b * 2 + (1 - c))

    def ag_drain(j):
        for dz in (1, 2, 3):
            ag_z(j, dz).wait_send()
        for zz in range(4):
            ag_y(j, zz).wait_send()
            for yy in range(2):
                ag_c(j, zz, yy).wait_send()

    def adapter(kind, dst, d):
        return remote(
            pool_hbm.at[:, 1 + kind, :, pl.ds(pl.multiple_of(d * 512, 512), 512)],
            dst.at[pl.ds(2 * me, 2)], ad_ss.at[kind, d], ad_rs.at[kind, me], d)

    def adapter_wait(kind, dst):
        loads[6 + kind].wait()

        def one(d):
            remote(
                pool_hbm.at[:, 1 + kind, :, pl.ds(0, 512)],
                dst.at[pl.ds(2 * d, 2)], ad_ss.at[kind, d], ad_rs.at[kind, d], d).wait_recv()
        peers(one)

    def spray(send, recv, ss, rs, per_peer):
        def one(d):
            src = send.at[d] if per_peer else send
            remote(src, recv.at[me], ss.at[d], rs.at[me], d).start()
        peers(one)

    def spray_wait(send, recv, ss, rs, per_peer):
        def one(d):
            src = send.at[d] if per_peer else send
            remote(src, recv.at[d], ss.at[d], rs.at[d], d).wait_recv()
        peers(one)

    def spray_drain(send, recv, ss, rs, per_peer):
        def one(d):
            src = send.at[d] if per_peer else send
            remote(src, recv.at[me], ss.at[d], rs.at[me], d).wait_send()
        peers(one)

    for j in range(CHUNKS):
        x_cur[j] = jnp.concatenate(
            [x0[:, q * QUARTER + j * LANES:q * QUARTER + (j + 1) * LANES].astype(F32) for q in range(4)],
            axis=0).astype(BF)
        ag_begin(j)
    peers(lambda d: adapter(0, bq, d).start())
    peers(lambda d: adapter(1, ao, d).start())

    col, line = jnp.zeros((64, 128), jnp.int32), jnp.zeros((8, 64), jnp.int32)
    for r in range(64):
        page = page_table[row_tenant[r]]
        col = jnp.where(iota((64, 128), 0) == r, page, col)
        line = jnp.where(iota((8, 64), 1) == r, page, line)
    for n in range(4):
        page_col[:, n * 128:(n + 1) * 128] = col
    page_row[...] = line

    def by_row(shape):
        got = jnp.zeros(shape, jnp.int32)
        for r in range(OWN):
            got = jnp.where((iota(shape, 0) & 3) == r, cache_length[r], got)
        return got
    lane = iota((16, 128), 1)
    frequency = jnp.exp((lane & 63).astype(F32) * (-2.0 / HD * math.log(rope_base)))
    for n in range(2):
        angle = (by_row((16, 128)) + n).astype(F32) * frequency
        cosine[n] = jnp.cos(angle)
        turned = jnp.sin(angle)
        sine[n] = jnp.where(lane < 64, -turned, turned)

    i, k = iota((256, 256), 0), iota((256, 256), 1)
    perm[...] = (k == ((i >> 2) & 15) * 16 + (i >> 6) * 4 + (i & 3)).astype(F32).astype(BF)
    perm_t[...] = (k == ((i >> 2) & 3) * 64 + (i >> 4) * 4 + (i & 3)).astype(F32).astype(BF)
    i, k = iota((512, 320), 0), iota((512, 320), 1)
    perm_q[...] = (k == ((i >> 2) & 7) * 64 + (i >> 5) * 4 + (i & 3)).astype(F32).astype(BF)
    qs_send[...] = jnp.zeros_like(qs_send)
    os_send[...] = jnp.zeros_like(os_send)
    kvbuf[pl.ds(KEYS, 256), :] = jnp.zeros((256, 256), BF)
    for part in range(4):
        keys = 384
        i, k = iota((256, keys), 0), iota((256, keys), 1)
        ok = ((i & 3) == part) & ((i >> 5) == (k & 7)) & ((k >> 3) < by_row((256, keys)))
        bias[:, pl.ds(part * keys, keys)] = jnp.where(ok, 0.0, -1e30)
    i, k = iota((256, 256), 0), iota((256, 256), 1)
    fresh = ((k & 15) == (i & 3)) & (((k >> 4) & 7) == (i >> 5))
    bias[:, pl.ds(KEYS, 256)] = jnp.where(fresh & (k < 128), 0.0, -1e30)

    for j in range(CHUNKS):
        ag_forward(j)
    for j in range(CHUNKS):
        ag_cross(j)
    loads[0].wait()
    loads[3].wait()

    def step(s, carry):
        @pl.when(s == 1)
        def _():
            i, k = iota((256, 256), 0), iota((256, 256), 1)
            fresh = ((k & 15) == (i & 3)) & (((k >> 4) & 7) == (i >> 5))
            bias[:, pl.ds(KEYS, 256)] = jnp.where(fresh, 0.0, -1e30)
            for j in range(CHUNKS):
                ag_forward(j)
            for j in range(CHUNKS):
                ag_cross(j)

        squares = jnp.zeros((64, 1), F32)
        shrink = jnp.zeros((32, 64), F32)
        for j in range(CHUNKS):
            ag_finish(j)
            xp[j] = dot(perm[...], xs[j].reshape(256, LANES)).astype(BF)
            for q in range(4):
                x = xp[j, q * 64:(q + 1) * 64, :]
                wide = x.astype(F32)
                squares += jnp.sum(wide * wide, axis=1, keepdims=True)
                a = aq[:, :, q * QUARTER + j * LANES:q * QUARTER + (j + 1) * LANES].reshape(32, LANES)
                shrink += dot_nt(a, x)
        here = page_row[0:1, :] == 2 * me + (iota((32, 64), 0) >> 4)
        shrink = jnp.where(here, shrink, 0.0)
        qs_send[:, 0:64] = (shrink[0:16] + shrink[16:32]).astype(BF)
        qs_recv[me] = qs_send[...]
        spray(qs_send, qs_recv, qs_ss, qs_rs, False)
        scale = lax.rsqrt(squares * (1.0 / 8192.0) + norm_epsilon)

        @pl.when(s == 0)
        def _():
            loads[1].wait()
            loads[2].wait()

        def project(n, acc):
            j, q = n // 4, n % 4
            x = xp[j, pl.ds(pl.multiple_of(q * 64, 64), 64), :]
            at = pl.ds(pl.multiple_of(q * QUARTER + j * LANES, LANES), LANES)
            return acc[0] + dot(x, wq[at, :]), acc[1] + dot(x, wkv[at, :])
        query, keyval = lax.fori_loop(
            0, 4 * CHUNKS, project, (jnp.zeros((64, 512), F32), jnp.zeros((64, 128), F32)))
        tq[pl.ds(256, 64), :] = (keyval * scale).astype(BF)

        spread_of = (iota((16, 512), 1) & 15) == iota((16, 512), 0)
        spread_of = spread_of.astype(F32).astype(BF)
        page_hit = page_col[...] == (iota((64, 512), 1) >> 4)

        @pl.when(s == 0)
        def _():
            adapter_wait(0, bq)
        spray_wait(qs_send, qs_recv, qs_ss, qs_rs, False)
        qs = jnp.sum(qs_recv[...].astype(F32), axis=0)
        low = dot(qs.T[0:64].astype(BF), spread_of)
        low = jnp.where(page_hit, low, 0.0).astype(BF)
        query = ((query + dot(low, bq[...].reshape(512, 512))) * scale).astype(BF)
        for h in range(4):
            tq[pl.ds(h * 64, 64), :] = query[:, h * 128:(h + 1) * 128]
        q_send[...] = dot(perm_q[...], tq[...]).astype(BF).reshape(16, 32, 128)
        q_recv[me] = q_send[me]
        spray(q_send, q_recv, q_ss, q_rs, True)
        spray_wait(q_send, q_recv, q_ss, q_rs, True)

        cos, sin = cosine[s], sine[s]

        def turn(v, n):
            flat = v.astype(F32).reshape(n * 16, 128)
            swapped = pltpu.roll(flat, 64, 1)
            both = flat.reshape(n, 16, 128) * cos[None] + swapped.reshape(n, 16, 128) * sin[None]
            return both.reshape(n * 16, 128).astype(BF)
        queries = turn(q_recv[:, 0:16, :], 16)
        fresh_kv = q_recv[:, 16:32, :].reshape(8, 2, 16, 128)
        new_at = pl.ds(pl.multiple_of(KEYS + 128 * s, 128), 128)
        kvbuf[new_at, 0:128] = turn(fresh_kv[:, 0], 8)
        kvbuf[new_at, 128:256] = fresh_kv[:, 1].reshape(128, 128)
        for half in range(2):
            rows = slice(half * 128, half * 128 + 128)
            score = dot_nt(queries[rows], kvbuf[:, 0:128]) * (float(HD) ** -0.5) + bias[rows, :]
            power = jnp.exp(score - jnp.max(score, axis=1, keepdims=True))
            total = jnp.sum(power, axis=1, keepdims=True)
            mixed = dot(power.astype(BF), kvbuf[:, 128:256]) / total
            a_send[half * 8:half * 8 + 8] = mixed.astype(BF).reshape(8, 16, 128)
        a_recv[me] = a_send[me]
        spray(a_send, a_recv, a_ss, a_rs, True)

        @pl.when(s == 0)
        def _():
            adapter_wait(1, ao)
            loads[4].wait()
            loads[5].wait()
        spray_wait(a_send, a_recv, a_ss, a_rs, True)

        heads = dot(perm[...], a_recv[...].reshape(256, 128)).astype(BF)
        for h in range(4):
            am[:, h * 128:(h + 1) * 128] = heads[h * 64:(h + 1) * 64]
        shrunk = dot_nt(ao[...].reshape(512, 512), am[...])
        shrunk = jnp.where(page_row[0:1, :] == (iota((512, 64), 0) >> 4), shrunk, 0.0)
        os_send[:, 0:64] = jnp.sum(shrunk.reshape(32, 16, 64), axis=0).astype(BF)
        os_recv[me] = os_send[...]
        spray(os_send, os_recv, os_ss, os_rs, False)

        def low_out():
            spray_wait(os_send, os_recv, os_ss, os_rs, False)
            os = jnp.sum(os_recv[...].astype(F32), axis=0)
            own = dot(os.T[0:64].astype(BF), spread_of[:, 0:32])
            mine = page_col[:, 0:32] == 2 * me + (iota((64, 32), 1) >> 4)
            return jnp.where(mine, own, 0.0).astype(BF)

        def rs1(j):
            return remote(bs.at[j, :, 1 - c], r1.at[j], rs1_ss.at[j], rs1_rs.at[j], c_peer)

        def rs2(j):
            return remote(s1.at[j, :, 1 - y], r2.at[j], rs2_ss.at[j], rs2_rs.at[j], y_peer)

        def rs3(j, dz):
            zz = lax.rem(z + dz, 4)
            return remote(s2.at[j, zz], r3.at[j, z], rs3_ss.at[j, dz], rs3_rs.at[j, z], zz * 4 + y * 2 + c)

        def rs3_wait(j, zz):
            remote(s2.at[j, zz], r3.at[j, zz], rs3_ss.at[j, 0], rs3_rs.at[j, zz], y_peer).wait_recv()

        for j in range(CHUNKS):
            ag_drain(j)
        def outward(n, carry):
            j, q = n // 4, n % 4
            at = pl.ds(pl.multiple_of(q * QUARTER + j * LANES, LANES), LANES)
            pw[pl.ds(pl.multiple_of(n * 64, 64), 64), :] = dot(am[...], wo[:, at])
            return carry
        lax.fori_loop(0, 4 * CHUNKS, outward, 0)
        spray_drain(qs_send, qs_recv, qs_ss, qs_rs, False)
        spray_drain(q_send, q_recv, q_ss, q_rs, True)
        spray_drain(a_send, a_recv, a_ss, a_rs, True)

        @pl.when(s == 1)
        def _():
            peers(lambda d: adapter(0, bq, d).wait_send())
            peers(lambda d: adapter(1, ao, d).wait_send())
        own = low_out()
        for j in range(CHUNKS):
            for q in range(4):
                n = j * 4 + q
                at = slice(q * QUARTER + j * LANES, q * QUARTER + (j + 1) * LANES)
                piece = pw[n * 64:(n + 1) * 64, :] + dot(own, bo[:, :, at].reshape(32, LANES))
                pb[q * 64:(q + 1) * 64, :] = piece.astype(BF)
            bs[j] = dot(perm_t[...], pb[...]).astype(BF).reshape(8, 2, 16, LANES)
            rs1(j).start()
        for j in range(CHUNKS):
            rs1(j).wait_recv()
            s1[j] = (bs[j, :, c].astype(F32) + r1[j].astype(F32)).astype(BF).reshape(4, 2, 16, LANES)
            rs2(j).start()
        for j in range(CHUNKS):
            rs2(j).wait_recv()
            s2[j] = (s1[j, :, y].astype(F32) + r2[j].astype(F32)).astype(BF)
            for dz in (1, 2, 3):
                rs3(j, dz).start()
        for j in range(CHUNKS):
            total = s2[j, z].astype(F32)
            for dz in (1, 2, 3):
                zz = lax.rem(z + dz, 4)
                rs3_wait(j, zz)
                total += r3[j, zz].astype(F32)
            update = total.astype(BF)
            out[s, j] = update
            x_cur[j] = (x_cur[j].astype(F32) + update.astype(F32)).astype(BF)

            @pl.when(s == 0)
            def _():
                ag_begin(j)
        for j in range(CHUNKS):
            rs1(j).wait_send()
            rs2(j).wait_send()
            for dz in (1, 2, 3):
                rs3(j, dz).wait_send()
        spray_drain(os_send, os_recv, os_ss, os_rs, False)
        return carry

    lax.fori_loop(0, 2, step, 0)


def on_device_fused(
    hidden_state, query_weight, keyval_weight, output_weight, cache_entries, adapter_pool,
    page_table, fetch_list, row_tenant, cache_length,
):
    vmem = pl.BlockSpec(memory_space=pltpu.VMEM)
    scalars = pl.BlockSpec(memory_space=pltpu.SMEM)
    anywhere = pl.BlockSpec(memory_space=pl.ANY)
    V = pltpu.VMEM
    D_ = pltpu.SemaphoreType.DMA
    result = pl.pallas_call(
        fused,
        out_shape=jax.ShapeDtypeStruct((2, CHUNKS, 16, LANES), BF),
        in_specs=[vmem] + [scalars] * 3 + [anywhere] * 5,
        out_specs=vmem,
        scratch_shapes=[
            V((8192, 512), BF), V((8192, 128), BF), V((512, 8192), BF),
            V((2, 16, 8192), BF), V((2, 16, 8192), BF), V((32, 16, 512), BF), V((32, 16, 512), BF),
            V((KEYS + 256, 256), BF), V((256, KEYS + 256), F32),
            V((256, 256), BF), V((256, 256), BF), V((512, 320), BF),
            V((64, 512), jnp.int32), V((8, 64), jnp.int32), V((2, 16, 128), F32), V((2, 16, 128), F32),
            V((CHUNKS, 16, LANES), BF), V((CHUNKS, 16, 16, LANES), BF), V((CHUNKS, 256, LANES), BF),
            V((CHUNKS * 256, LANES), F32), V((256, LANES), BF), V((CHUNKS, 8, 2, 16, LANES), BF),
            V((CHUNKS, 8, 16, LANES), BF), V((CHUNKS, 4, 2, 16, LANES), BF),
            V((CHUNKS, 4, 16, LANES), BF), V((CHUNKS, 4, 16, LANES), BF), V((CHUNKS, 4, 16, LANES), BF),
            V((16, 128), BF), V((16, 16, 128), BF), V((320, 128), BF),
            V((16, 32, 128), BF), V((16, 32, 128), BF),
            V((16, 16, 128), BF), V((16, 16, 128), BF), V((64, 512), BF),
            V((16, 128), BF), V((16, 16, 128), BF),
            D_((8,)), D_((2, 16)), D_((2, 16)), D_((CHUNKS, 4)), D_((CHUNKS, 4)), D_((CHUNKS, 8)),
            D_((CHUNKS, 16)),
            D_((16,)), D_((16,)), D_((16,)), D_((16,)), D_((16,)), D_((16,)), D_((16,)), D_((16,)),
            D_((CHUNKS,)), D_((CHUNKS,)), D_((CHUNKS,)), D_((CHUNKS,)), D_((CHUNKS, 4)), D_((CHUNKS, 4)),
        ],
        compiler_params=pltpu.CompilerParams(
            collective_id=0, has_side_effects=True, vmem_limit_bytes=56 * 1024 * 1024),
    )(
        hidden_state, page_table, row_tenant, cache_length,
        query_weight, keyval_weight, output_weight, cache_entries.reshape(KEYS, 2 * HD), adapter_pool,
    )
    result = result.reshape(2, CHUNKS, 4, OWN, LANES).transpose(0, 3, 2, 1, 4)
    return result.reshape(2, OWN, 4 * QUARTER)


def solution(mesh):
    local = on_device
    if mesh.shape["tensor"] == DEVS and mesh.shape["pool"] == 1:
        local = on_device_fused
    return jax.shard_map(
        local,
        mesh=mesh,
        in_specs=(
            P(("groups", "pool", "tensor"), None),
            P(None, "tensor"),
            P(None, "tensor"),
            P("tensor", None),
            P(("groups", "pool", "tensor"), None, None, None),
            P(("groups", "pool", "tensor"), None, None, None),
            P("groups"),
            P("groups"),
            P(("groups", "pool")),
            P(("groups", "pool", "tensor")),
        ),
        out_specs=P(None, ("groups", "pool", "tensor"), None),
        check_vma=False,
    )
```
